256 devices in a mesh: dir: 8 (over x, core), sx: 4 (over y), sy: 8 (over z).
Axes of the slice: x: 4, y: 4, z: 8, core: 2. Of those that a mesh axis runs over, the one named last changes fastest.
Arguments:
- signs_x: int32 [8, 256], P('dir', 'sx'), may hold values from -2147483648 to 2147483647, as said below
- signs_y: int32 [8, 1024], P('dir', 'sy'), may hold values from -2147483648 to 2147483647, as said below
- heights: int32 [256, 1024], P('sx', 'sy'), may hold values from 0 to 63
- velocity: float32 [256, 1024], P('sx', 'sy'), may hold values from 1 to 2
- background: float32 [8, 256, 1024], P('dir', 'sx', 'sy'), may hold values from -4 to 4
Outputs:
- basis: float32 [256, 256, 1024], P('dir', 'sx', 'sy')
- factor: float32 [256, 256], P('dir')
The draws below stay inside these ranges and needn't reach their ends.
Inputs may be any that keep to these rules, and one draw needn't show every extreme that they name: `signs_x`: packed sign words, every bit pattern possible. `signs_y`: packed sign words, every bit pattern possible.
All inputs are finite; a program needn't handle non-finite values.
Results may differ from the reference program's by a relative error of at most 0.00027.
Values sent between devices are 32-bit elements; how exact they have to be, the bound alone decides.
No kernel may reach another device: no remote copies, remote signals or barrier semaphores. Data moves between devices by JAX's collectives and lax.ppermute only.
A program may use at most 64 MiB of HBM per device.

```python
import math
import jax
import jax.numpy as jnp
from jax import lax

PROBES = 32
LEVELS = 64
SHOTS = 8
DIRS = 256
NX = 256
NY = 1024
N_DIR = 8


def packed_words(key, salt, length, flip_terms):
    base_words = jax.random.randint(jax.random.fold_in(key, salt), (1, length), -2147483648, 2147483647, dtype=jnp.int32)
    flips = jax.random.randint(jax.random.fold_in(key, salt + 1), (SHOTS, length), -2147483648, 2147483647, dtype=jnp.int32)
    for extra in range(flip_terms - 1):
        more = jax.random.randint(jax.random.fold_in(key, salt + 2 + extra), (SHOTS, length), -2147483648, 2147483647, dtype=jnp.int32)
        flips = flips & more
    return jnp.bitwise_xor(base_words, flips)


def draw_signs_x(key, part):
    return packed_words(key, 101, NX, 2)


def draw_signs_y(key, part):
    return packed_words(key, 211, NY, 3)


def draw_background(key, part):
    common_key = jax.random.fold_in(key, 307)
    own_key = jax.random.fold_in(key, 311)
    common = jax.random.normal(common_key, (1, NX, NY), jnp.float32)
    own = jax.random.normal(own_key, (SHOTS, NX, NY), jnp.float32)
    mixed = 0.8 * common + 0.6 * own
    return jnp.clip(mixed, -4.0, 4.0).astype(jnp.float32)


def place_ends(result, key, smallest, largest):
    longest = result.shape.index(max(result.shape))
    spots = []
    for shift in (0, 1):
        where = [jax.random.randint(jax.random.fold_in(key, axis), (), 0, length) for axis, length in enumerate(result.shape)]
        where[longest] = (where[longest] + shift) % result.shape[longest]
        spots.append(tuple(where))
    return result.at[spots[0]].set(smallest).at[spots[1]].set(largest)


def steps_of(key, dims, split, low, high):
    loudness = 1.0
    for axis_at, blocks in split:
        steps = jax.random.uniform(jax.random.fold_in(jax.random.fold_in(key, 6), axis_at), (blocks,), jnp.float32, low / len(split), high / len(split))
        loudness = loudness * jnp.repeat(jnp.exp(steps), dims[axis_at] // blocks).reshape((-1,) + (1,) * (len(dims) - 1 - axis_at))
    return loudness


def setup_inputs(seed: int = 0) -> dict:
    streams_of = jax.random.split(jax.random.key(seed), 6)
    return {
        "signs_x": draw_signs_x(jax.random.fold_in(streams_of[5], 71), 0),
        "signs_y": draw_signs_y(jax.random.fold_in(streams_of[5], 71), 0),
        "heights": place_ends(jax.random.randint(streams_of[2], (NX, NY), 0, LEVELS), jax.random.fold_in(streams_of[2], 1), 0, LEVELS - 1).astype(jnp.int32),
        "velocity": jnp.clip(jnp.exp(math.log(2.0) - 0.6931472 * jax.random.uniform(streams_of[3], (NX, NY), jnp.float32) ** steps_of(streams_of[3], (NX, NY), ((0, 4), (1, 8)), -0.2, 0.2)), 1.0, 2.0),
        "background": draw_background(jax.random.fold_in(streams_of[5], 71), 0),
    }


tau_step = 0.02

def unpack_signs(packed, per_group):
    bit_index = jnp.arange(per_group, dtype=jnp.int32)
    bit_values = jnp.right_shift(packed[:, None, :], bit_index[None, :, None]) & 1
    signed = (2 * bit_values - 1).astype(jnp.float32)
    return signed.reshape(packed.shape[0] * per_group, packed.shape[1])

def apply_step(wavefield, stiffness):
    weighted = stiffness * wavefield
    padded = jnp.pad(weighted, ((0, 0), (1, 1), (1, 1)))
    laplace = padded[:, 2:, 1:-1] + padded[:, :-2, 1:-1] + padded[:, 1:-1, 2:] + padded[:, 1:-1, :-2] - 4.0 * weighted
    return wavefield + tau_step * stiffness * laplace

def reference(signs_x, signs_y, heights, velocity, background):
    first_signs = unpack_signs(signs_x, PROBES)
    second = unpack_signs(signs_y, PROBES)
    kronecker = first_signs[:, :, None] * second[:, None, :]
    rolled = jnp.roll(kronecker.reshape(N_DIR, PROBES, NX, NY), -1, axis=1).reshape(DIRS, NX, NY)
    probe_dirs = kronecker + 0.5 * rolled
    stiffness = velocity * jnp.sqrt(1.0 + heights.astype(jnp.float32) / LEVELS)
    shot_fields = jnp.repeat(background, PROBES, axis=0)
    wavefield = shot_fields * probe_dirs
    for repeat in range(4):
        wavefield = apply_step(wavefield, stiffness[None])
    response = (shot_fields * wavefield).reshape(DIRS, NX * NY)
    gram_matrix = jnp.dot(response.astype(jnp.float32), response.T.astype(jnp.float32), precision=lax.Precision.HIGHEST, preferred_element_type=jnp.float32)
    factor_low = jnp.linalg.cholesky(gram_matrix)
    orthonormal = lax.linalg.triangular_solve(factor_low, response, left_side=True, lower=True)
    cell_count = math.sqrt(NX * NY)
    basis = (orthonormal * cell_count).reshape(DIRS, NX, NY)
    factor = factor_low.T / cell_count
    return (basis, factor)
```

```python
import functools
import math

import jax
import jax.numpy as jnp
from jax import lax
from jax.experimental import pallas as pl
from jax.experimental.pallas import tpu as pltpu
from jax.sharding import PartitionSpec as P

PROBES = 32
LEVELS = 64
HALO = 4
ROWS = 8
tau_step = 0.02

F32 = jnp.float32
BF16 = jnp.bfloat16
TN = (((0,), (0,)), ((), ()))
NT = (((1,), (1,)), ((), ()))


def split2(x):
    high = x.astype(BF16)
    return high, (x - high.astype(F32)).astype(BF16)


def split3(x):
    high = x.astype(BF16).astype(F32)
    rest = x - high
    mid = rest.astype(BF16).astype(F32)
    return high, mid, rest - mid


def response_kernel(shots, nx, ny, field_ref, stiff_ref, gram_ref, high_ref, low_ref,
                    first, first_next, second, second_next, coef, w0, w1, w2, w3, total):
    dirs = shots * PROBES
    ext_x, ext_y = nx + 2 * HALO, ny + 2 * HALO
    step = pl.program_id(0)

    @pl.when(step == 0)
    def _():
        total[...] = jnp.zeros_like(total)
        words = jnp.concatenate(
            [field_ref[g, ext_x:ext_x + 8, :] for g in range(shots)], axis=0
        ).astype(BF16)
        row = lax.broadcasted_iota(jnp.int32, (8 * shots, dirs), 0)
        col = lax.broadcasted_iota(jnp.int32, (8 * shots, dirs), 1)

        def bits(offset, shift):
            probe = (col + shift) % PROBES
            pick = (row // 8 == col // PROBES) & (row % 8 - offset == probe // 8)
            value = lax.dot_general(words, jnp.where(pick, 1.0, 0.0).astype(BF16), TN, preferred_element_type=F32)
            lane = (lax.broadcasted_iota(jnp.int32, value.shape, 1) + shift) % 8
            bit = jnp.right_shift(value.astype(jnp.int32), lane) & 1
            return (2 * bit - 1).astype(F32)

        first[...] = bits(0, 0)[:ext_x]
        first_next[...] = 0.5 * bits(0, 1)[:ext_x]
        second[...] = bits(4, 0)
        second_next[...] = bits(4, 1)

    row = lax.broadcasted_iota(jnp.int32, (32, dirs + 128), 0)
    col = lax.broadcasted_iota(jnp.int32, (32, dirs + 128), 1)
    in_shot = (row < 24) & (row % 8 == col // PROBES) & (col < dirs)
    in_coef = (row >= 24) & (row < 27) & (col >= dirs)
    expand = jnp.where(in_shot | in_coef, 1.0, 0.0).astype(BF16)
    sub = lax.broadcasted_iota(jnp.int32, (8, ext_y), 0)

    def stencil(src, row_at, dst):
        up, mid, down = (row_at - 1) & 3, row_at & 3, (row_at + 1) & 3
        c = coef[row_at & 7]
        out = []
        for h in range(dirs // 128):
            lanes = slice(128 * h, 128 * h + 128)
            w = src[mid, :, lanes]
            around = (src[up, :, lanes] + src[down, :, lanes]) + (
                pltpu.roll(w, 1, 0) + pltpu.roll(w, ext_y - 1, 0)
            )
            new = w + c * (around - 4.0 * w)
            if dst is not None:
                dst[mid, :, lanes] = new
            out.append(new)
        return out

    for k in range(ROWS):
        i = step * ROWS + k
        s_row = stiff_ref[pl.ds(i, 1), :]
        shot_rows = jnp.concatenate([field_ref[g, pl.ds(i, 1), :] for g in range(shots)], axis=0)
        c3 = split3(tau_step * s_row * s_row)
        c_rows = jnp.where(sub == 0, c3[0], jnp.where(sub == 1, c3[1], jnp.where(sub == 2, c3[2], 0.0)))
        lhs = jnp.concatenate([*split3(shot_rows * s_row), c_rows], axis=0).astype(BF16)
        wide = lax.dot_general(lhs, expand, TN, preferred_element_type=F32)
        coef[i & 7] = wide[:, dirs:]
        probe = first[pl.ds(i, 1), :] * second[...] + first_next[pl.ds(i, 1), :] * second_next[...]
        w0[i & 3] = wide[:, :dirs] * probe
        stencil(w0, i - 1, w1)
        stencil(w1, i - 2, w2)
        stencil(w2, i - 3, w3)
        last = stencil(w3, i - 4, None)
        at = jnp.maximum(i - HALO, 0)
        s_row = stiff_ref[pl.ds(at, 1), :]
        shot_rows = jnp.concatenate([field_ref[g, pl.ds(at, 1), :] for g in range(shots)], axis=0)
        scale = shot_rows / jnp.where(s_row > 0.0, s_row, 1.0)
        lhs = jnp.concatenate([*split3(scale), jnp.zeros_like(scale)], axis=0).astype(BF16)
        wide = lax.dot_general(lhs, expand[:, :dirs], TN, preferred_element_type=F32)
        for h in range(dirs // 128):
            lanes = slice(128 * h, 128 * h + 128)
            value = (last[h] * wide[:, lanes])[HALO:HALO + ny]
            high_ref[k, :, lanes], low_ref[k, :, lanes] = split2(value)

    @pl.when(step > 0)
    def _():
        high = high_ref[...].reshape(ROWS * ny, dirs)
        low = low_ref[...].reshape(ROWS * ny, dirs)
        total[:, :dirs] += lax.dot_general(high, high, TN, preferred_element_type=F32)
        total[:, dirs:] += lax.dot_general(high, low, TN, preferred_element_type=F32)

    @pl.when(step == pl.num_programs(0) - 1)
    def _():
        cross = total[:, dirs:]
        gram_ref[...] = total[:, :dirs] + cross + cross.T


def responses(fields, stiffness, shots, nx, ny):
    dirs = shots * PROBES
    ext_x, ext_y = nx + 2 * HALO, ny + 2 * HALO
    whole = lambda shape: pl.BlockSpec(shape, lambda s: (0,) * len(shape))
    block = pl.BlockSpec((ROWS, ny, dirs), lambda s: (jnp.maximum(s - 1, 0), 0, 0))
    return pl.pallas_call(
        functools.partial(response_kernel, shots, nx, ny),
        grid=(ext_x // ROWS,),
        in_specs=[whole(fields.shape), whole(stiffness.shape)],
        out_specs=[whole((dirs, dirs)), block, block],
        out_shape=[
            jax.ShapeDtypeStruct((dirs, dirs), F32),
            jax.ShapeDtypeStruct((nx, ny, dirs), BF16),
            jax.ShapeDtypeStruct((nx, ny, dirs), BF16),
        ],
        scratch_shapes=[
            pltpu.VMEM((ext_x, dirs), F32),
            pltpu.VMEM((ext_x, dirs), F32),
            pltpu.VMEM((ext_y, dirs), F32),
            pltpu.VMEM((ext_y, dirs), F32),
            pltpu.VMEM((8, ext_y, 128), F32),
            *[pltpu.VMEM((4, ext_y, dirs), F32) for _ in range(4)],
            pltpu.VMEM((dirs, 2 * dirs), F32),
        ],
        compiler_params=pltpu.CompilerParams(
            dimension_semantics=("arbitrary",), vmem_limit_bytes=48 * 2**20
        ),
        name="responses",
    )(fields, stiffness)


PANEL = 64
PIVOT = 4


def cholesky_kernel(n, scale, strip, index_ref, gram_ref, upper_ref, inverse_ref, table):
    tiles = n // 128
    groups = n // 8
    eye_row = lax.broadcasted_iota(jnp.int32, (8, 128), 0)
    eye_col = lax.broadcasted_iota(jnp.int32, (8, 128), 1)
    table[:, :n] = gram_ref[...]
    full = lambda x: jnp.broadcast_to(x, (8, 128))
    for panel in range(n // PANEL):
        start = panel * PANEL
        tile = start // 128
        live = [*range(tile, tiles), *range(tiles, tiles + tile + 1)]
        rows = {}
        for g in range(PANEL // 8):
            for t in live:
                at = start + 8 * g
                value = None
                if t < tiles or panel > 0:
                    value = table[at:at + 8, 128 * t:128 * t + 128] if (t < tiles or (t - tiles) * 128 < start) else None
                if t >= tiles:
                    unit = (eye_row + at == eye_col + 128 * (t - tiles)).astype(F32)
                    value = unit if value is None else value + unit
                rows[g, t] = value
        for micro in range(PANEL // PIVOT):
            k = micro * PIVOT
            gp, r = k // 8, k % 8
            lane = (start + k) % 128
            pivot_rows = [{t: full(rows[gp, t][r + j:r + j + 1, :]) for t in live} for j in range(PIVOT)]
            a = {
                (i, j): full(pivot_rows[i][tile][:, lane + j:lane + j + 1])
                for i in range(PIVOT) for j in range(i + 1)
            }
            low, inv = {}, []
            for j in range(PIVOT):
                d = a[j, j]
                for m in range(j):
                    d = d - low[j, m] * low[j, m]
                inv.append(lax.rsqrt(d))
                for i in range(j + 1, PIVOT):
                    v = a[i, j]
                    for m in range(j):
                        v = v - low[i, m] * low[j, m]
                    low[i, j] = v * inv[j]
            ready = []
            for j in range(PIVOT):
                out = {}
                for t in live:
                    v = pivot_rows[j][t]
                    for m in range(j):
                        v = v - low[j, m] * ready[m][t]
                    out[t] = v * inv[j]
                ready.append(out)
            for g in range(gp, PANEL // 8):
                if g == gp and r + PIVOT == 8:
                    pass
                else:
                    cols = []
                    for j in range(PIVOT):
                        v = full(rows[g, tile][:, lane + j:lane + j + 1])
                        for m in range(j):
                            v = v - cols[m] * low[j, m]
                        cols.append(v * inv[j])
                    if g == gp:
                        cols = [jnp.where(eye_row >= r + PIVOT, v, 0.0) for v in cols]
                    for t in live:
                        v = rows[g, t]
                        for j in range(PIVOT):
                            v = v - cols[j] * ready[j][t]
                        rows[g, t] = v
                if g == gp:
                    for t in live:
                        v = rows[g, t]
                        for j in range(PIVOT):
                            v = jnp.where(eye_row == r + j, ready[j][t], v)
                        rows[g, t] = v
        for g in range(PANEL // 8):
            for t in live:
                at = start + 8 * g
                value = rows[g, t]
                if t == tile:
                    value = jnp.where(eye_row + at <= eye_col + 128 * t, value, 0.0)
                table[at:at + 8, 128 * t:128 * t + 128] = value
            for t in range(tile):
                table[start + 8 * g:start + 8 * g + 8, 128 * t:128 * t + 128] = jnp.zeros((8, 128), F32)
            for t in range(tiles + tile + 1, 2 * tiles):
                table[start + 8 * g:start + 8 * g + 8, 128 * t:128 * t + 128] = jnp.zeros((8, 128), F32)
        below = start + PANEL
        if below < n:
            keep = below // 128
            for t in range(keep, tiles + tile + 1):
                if t == keep:
                    lo = 128 * keep
                    left = table[start:below, lo:n]
                    p3 = [v.astype(BF16) for v in split3(left)]
                    lhs = jnp.concatenate([p3[0], p3[0], p3[1], p3[0], p3[2], p3[1]], axis=0)
                lanes = slice(128 * t, 128 * t + 128)
                right = [v.astype(BF16) for v in split3(table[start:below, lanes])]
                rhs = jnp.concatenate([right[0], right[1], right[0], right[2], right[0], right[1]], axis=0)
                update = lax.dot_general(lhs, rhs, TN, preferred_element_type=F32)[below - lo:]
                if t < tiles or 128 * (t - tiles) < start:
                    table[below:, lanes] = table[below:, lanes] - update
                else:
                    table[below:, lanes] = -update
    own = pl.ds(pl.multiple_of(index_ref[0] * strip, strip), strip)
    upper_ref[...] = table[own, :n] * (1.0 / scale)
    inverse_ref[...] = table[own, n:] * scale


def factorise(gram, index, scale, strip):
    n = gram.shape[0]
    return pl.pallas_call(
        functools.partial(cholesky_kernel, n, scale, strip),
        in_specs=[pl.BlockSpec(memory_space=pltpu.SMEM), pl.BlockSpec(memory_space=pltpu.VMEM)],
        out_specs=[pl.BlockSpec(memory_space=pltpu.VMEM)] * 2,
        out_shape=[jax.ShapeDtypeStruct((strip, n), F32)] * 2,
        scratch_shapes=[pltpu.VMEM((n, 2 * n), F32)],
        compiler_params=pltpu.CompilerParams(vmem_limit_bytes=32 * 2**20),
        name="factorise",
    )(index, gram)


def basis_kernel(inverse_ref, high_ref, low_ref, out_ref):
    strip = inverse_ref.shape[0]
    high, low = split2(inverse_ref[...])
    both = jnp.concatenate([high, low], axis=0)
    for i in range(high_ref.shape[0]):
        main = lax.dot_general(both, high_ref[i], NT, preferred_element_type=F32)
        rest = lax.dot_general(high, low_ref[i], NT, preferred_element_type=F32)
        out_ref[:, i, :] = main[:strip] + (main[strip:] + rest)


def project(inverse, high, low):
    nx, ny, dirs = high.shape
    strip = inverse.shape[0]
    block = pl.BlockSpec((ROWS, ny, dirs), lambda s: (s, 0, 0))
    return pl.pallas_call(
        basis_kernel,
        grid=(nx // ROWS,),
        in_specs=[pl.BlockSpec(inverse.shape, lambda s: (0, 0)), block, block],
        out_specs=pl.BlockSpec((strip, ROWS, ny), lambda s: (0, s, 0)),
        out_shape=jax.ShapeDtypeStruct((strip, nx, ny), F32),
        compiler_params=pltpu.CompilerParams(
            dimension_semantics=("arbitrary",), vmem_limit_bytes=32 * 2**20
        ),
        name="project",
    )(inverse, high, low)


def edges(value, axis, dim):
    count = lax.axis_size(axis)
    size = value.shape[dim]
    head = lax.slice_in_dim(value, 0, HALO, axis=dim)
    tail = lax.slice_in_dim(value, size - HALO, size, axis=dim)
    before = lax.ppermute(tail, axis, [(i, i + 1) for i in range(count - 1)])
    after = lax.ppermute(head, axis, [(i + 1, i) for i in range(count - 1)])
    return jnp.concatenate([before, value, after], axis=dim)


def as_bytes(words):
    shifts = 8 * jnp.arange(4, dtype=jnp.int32)
    return (jnp.right_shift(words[None, :], shifts[:, None]) & 255).astype(F32)


def shards(signs_x, signs_y, heights, velocity, background):
    shots = lax.axis_size("dir")
    nx, ny = background.shape[1:]
    ext_x, ext_y = nx + 2 * HALO, ny + 2 * HALO
    stiffness = velocity * jnp.sqrt(1.0 + heights.astype(F32) / LEVELS)
    bytes_x = jnp.pad(as_bytes(signs_x[0]).T, ((0, 0), (0, ny - 4)))
    packed = edges(jnp.stack([background[0], stiffness, bytes_x]), "sx", 1)
    bytes_x = packed[2, :, :4].T
    packed = jnp.concatenate([packed[:2].reshape(2 * ext_x, ny), as_bytes(signs_y[0])], axis=0)
    packed = edges(packed, "sy", 1)
    stiffness = packed[ext_x:2 * ext_x]
    own = jnp.concatenate(
        [packed[:ext_x], jnp.pad(bytes_x, ((0, 0), (0, ext_y - ext_x))), packed[2 * ext_x:]], axis=0
    )
    fields = lax.all_to_all(jnp.broadcast_to(own[None], (shots, *own.shape)), "dir", 0, 0)
    gram, high, low = responses(fields, stiffness, shots, nx, ny)
    dirs = shots * PROBES
    index = lax.axis_index("dir")
    strip = lax.dynamic_slice_in_dim(gram, index * PROBES, PROBES, 0)
    terms = lax.all_to_all(strip.reshape(PROBES, dirs // 128, 128), ("sx", "sy"), 0, 0)
    row = jnp.sum(terms, axis=0, keepdims=True)
    gram = lax.all_to_all(jnp.broadcast_to(row, (dirs, *row.shape[1:])), ("dir", "sx", "sy"), 0, 0)
    gram = gram.reshape(dirs, dirs)
    scale = math.sqrt(nx * ny * lax.axis_size("sx") * lax.axis_size("sy"))
    factor, inverse = factorise(gram, index.reshape(1), scale, PROBES)
    return project(inverse, high, low), factor


def solution(mesh):
    in_specs = (P("dir", "sx"), P("dir", "sy"), P("sx", "sy"), P("sx", "sy"), P("dir", "sx", "sy"))
    out_specs = (P("dir", "sx", "sy"), P("dir", None))
    return jax.shard_map(shards, mesh=mesh, in_specs=in_specs, out_specs=out_specs, check_vma=False)
```

```python
import functools
import math

import jax
import jax.numpy as jnp
from jax import lax
from jax.experimental import pallas as pl
from jax.experimental.pallas import tpu as pltpu
from jax.sharding import PartitionSpec as P

PROBES = 32
LEVELS = 64
HALO = 4
ROWS = 8
tau_step = 0.02

F32 = jnp.float32
BF16 = jnp.bfloat16
TN = (((0,), (0,)), ((), ()))
NT = (((1,), (1,)), ((), ()))
VMEM = pl.BlockSpec(memory_space=pltpu.VMEM)
SMEM = pl.BlockSpec(memory_space=pltpu.SMEM)
HBM = pl.BlockSpec(memory_space=pltpu.HBM)


def split2(x):
    high = x.astype(BF16)
    return high, (x - high.astype(F32)).astype(BF16)


def split3(x):
    high = x.astype(BF16).astype(F32)
    rest = x - high
    mid = rest.astype(BF16).astype(F32)
    return high, mid, rest - mid


def sign_bytes(words):
    shape = (8, words.shape[1])
    shift = 8 * (lax.broadcasted_iota(jnp.int32, shape, 0) & 3)
    return (jnp.right_shift(jnp.broadcast_to(words, shape), shift) & 255).astype(F32)


def pack_x_kernel(signs_ref, heights_ref, velocity_ref, field_ref, stiff_ref, first_ref, last_ref):
    nx, ny = velocity_ref.shape
    stiff = velocity_ref[...] * jnp.sqrt(1.0 + heights_ref[...].astype(F32) / LEVELS)
    stiff_ref[...] = stiff
    octets = sign_bytes(signs_ref[...])
    for ref, start in ((first_ref, 0), (last_ref, nx - HALO)):
        ref[0:HALO, :] = field_ref[0, start:start + HALO, :]
        ref[HALO:2 * HALO, :] = stiff[start:start + HALO]
        ref[8:16, :] = jnp.zeros((8, ny), F32)
        ref[8:16, :nx] = octets


def pack_y_kernel(signs_ref, field_ref, stiff_ref, own_ref, above_ref, below_ref,
                  field_out, stiff_out, octets_out, first_ref, last_ref):
    nx, ny = stiff_ref.shape
    ext_x = nx + 2 * HALO
    field_out[0:HALO, :] = above_ref[0:HALO, :]
    field_out[HALO:HALO + nx, :] = field_ref[0]
    field_out[HALO + nx:ext_x, :] = below_ref[0:HALO, :]
    stiff_out[0:HALO, :] = above_ref[HALO:2 * HALO, :]
    stiff_out[HALO:HALO + nx, :] = stiff_ref[...]
    stiff_out[HALO + nx:ext_x, :] = below_ref[HALO:2 * HALO, :]
    lane = lax.broadcasted_iota(jnp.int32, (8, ny), 1)
    after = pltpu.roll(below_ref[8:16, :], nx + HALO, 1)
    before = pltpu.roll(above_ref[8:16, :], ny - nx + HALO, 1)
    own = pltpu.roll(own_ref[8:16, :], HALO, 1)
    octets_out[...] = jnp.where(lane < HALO, before, jnp.where(lane < HALO + nx, own, after))
    octets = sign_bytes(signs_ref[...])
    field, stiff = field_out[...], stiff_out[...]
    lane = lax.broadcasted_iota(jnp.int32, field.shape, 1)
    first_ref[0:ext_x, :] = jnp.where(lane < HALO, field, pltpu.roll(stiff, HALO, 1))
    first_ref[ext_x:, :] = octets
    last_ref[0:ext_x, :] = jnp.where(lane < 2 * HALO, pltpu.roll(field, 2 * HALO, 1), pltpu.roll(stiff, 3 * HALO, 1))
    last_ref[ext_x:, :] = octets


def pack_dir_kernel(index_ref, field_ref, stiff_ref, octets_ref, own_ref, left_ref, right_ref, send_ref, stiff_out):
    ext_x, ny = field_ref.shape
    half = (ext_x - 2 * HALO) // 2
    take = half + 2 * HALO
    left, right = left_ref[0:ext_x, :], right_ref[0:ext_x, :]
    lane = lax.broadcasted_iota(jnp.int32, left.shape, 1)
    field_side = jnp.where(lane < HALO, right, left)
    shift = lambda v: pltpu.roll(v, ny - HALO, 1)
    stiff_side = jnp.where(lane < HALO, shift(right), shift(left))
    lane = lax.broadcasted_iota(jnp.int32, (8, ny), 1)
    octet_side = jnp.where(lane < HALO, right_ref[ext_x:, :], pltpu.roll(left_ref[ext_x:, :], 2 * HALO, 1))
    own_octets = own_ref[ext_x:, :]
    for dest in range(send_ref.shape[0]):
        part = dest & 1
        rows = slice(part * half, part * half + take)
        send_ref[dest, 0:take, 0:ny] = field_ref[rows, :]
        send_ref[dest, 0:take, ny:] = field_side[rows, :2 * HALO]
        x_octets = octets_ref[...] if part == 0 else pltpu.roll(octets_ref[...], ny - half, 1)
        send_ref[dest, take:take + 4, 0:ny] = x_octets[0:4]
        send_ref[dest, take:take + 4, ny:] = jnp.zeros((4, 2 * HALO), F32)
        send_ref[dest, take + 4:take + 8, 0:ny] = own_octets[0:4]
        send_ref[dest, take + 4:take + 8, ny:] = octet_side[0:4, :2 * HALO]
    row = pl.multiple_of((index_ref[0] & 1) * half, half)
    stiff_out[:, 0:ny] = stiff_ref[pl.ds(row, take), :]
    spare = jnp.where(index_ref[0] & 1 == 1, stiff_side[half:half + take], stiff_side[0:take])
    stiff_out[:, ny:] = spare[:, :2 * HALO]


def small(kernel, shapes, specs, name):
    return pl.pallas_call(
        kernel,
        in_specs=specs,
        out_specs=[VMEM] * len(shapes),
        out_shape=[jax.ShapeDtypeStruct(shape, F32) for shape in shapes],
        name=name,
    )


def exchange(first, last, axis):
    count = lax.axis_size(axis)
    before = lax.ppermute(last, axis, [(i, i + 1) for i in range(count - 1)])
    after = lax.ppermute(first, axis, [(i + 1, i) for i in range(count - 1)])
    return before, after


PART = 32


def response_kernel(shots, nx, ny, index_ref, field_ref, stiff_ref, own_ref, other_ref, high_ref, low_ref,
                    expand, stack, spread, first, first_next, second, second_next,
                    coef, back, field, w0, w1, w2, w3, fold, total):
    dirs = shots * PROBES
    halves = dirs // 128
    ext_x, ext_y = nx + 2 * HALO, ny + 2 * HALO
    depth = ext_y // 8
    width = dirs + 256
    step = pl.program_id(0)

    @pl.when(step == 0)
    def _():
        total[...] = jnp.zeros_like(total)
        row = lax.broadcasted_iota(jnp.int32, (2 * PART, 2 * width), 0)
        col = lax.broadcasted_iota(jnp.int32, (2 * PART, 2 * width), 1)
        same = row // PART == col // width
        row, col = row % PART, col % width
        pick = (row < 24) & (row % 8 == col // PROBES) & (col < dirs)
        pick |= (row >= 24) & (row < 27) & (col >= dirs) & (col < dirs + 128)
        pick |= (row >= 27) & (row < 30) & (col >= dirs + 128)
        expand[...] = jnp.where(pick & same, 1.0, 0.0).astype(BF16)
        s = stiff_ref[...]
        stack[...] = jnp.zeros_like(stack)

        def put(value, at):
            where = pl.ds(at, ext_x, PART)
            stack[0, where, :] = value[:, :128]
            stack[1, where, :] = jnp.concatenate([value[:, 128:], jnp.zeros((ext_x, 256 - ext_y), F32)], axis=1)

        for g in range(shots):
            for part, value in enumerate(split3(field_ref[g, :ext_x, :] * s)):
                put(value, 8 * part + g)
        square = s * s
        for part, value in enumerate(split3(tau_step * square)):
            put(value, 24 + part)
        for part, value in enumerate(split3(1.0 / jnp.where(s > 0.0, square, 1.0))):
            put(value, 27 + part)
        words = jnp.concatenate(
            [field_ref[g, ext_x:ext_x + 8, :] for g in range(shots)], axis=0
        ).astype(BF16)
        row = lax.broadcasted_iota(jnp.int32, (8 * shots, dirs), 0)
        col = lax.broadcasted_iota(jnp.int32, (8 * shots, dirs), 1)

        def bits(offset, shift):
            probe = (col + shift) % PROBES
            hit = (row // 8 == col // PROBES) & (row % 8 - offset == probe // 8)
            value = lax.dot_general(words, jnp.where(hit, 1.0, 0.0).astype(BF16), TN, preferred_element_type=F32)
            lane = (lax.broadcasted_iota(jnp.int32, value.shape, 1) + shift) % 8
            bit = jnp.right_shift(value.astype(jnp.int32), lane) & 1
            return (2 * bit - 1).astype(F32)

        first[...] = bits(0, 0)[:ext_x]
        first_next[...] = 0.5 * bits(0, 1)[:ext_x]
        for ref, shift in ((second, 0), (second_next, 1)):
            value = bits(4, shift)
            for h in range(halves):
                spread[h] = value[:, 128 * h:128 * h + 128]
                for v in range(depth):
                    ref[h, v] = spread[h, pl.ds(v, 8, depth), :]

    def around(w):
        after = jnp.concatenate([w[1:], pltpu.roll(w[0], 7, 0)[None]], axis=0)
        before = jnp.concatenate([pltpu.roll(w[depth - 1], 1, 0)[None], w[:depth - 1]], axis=0)
        return after + before

    def stencil(src, at, dst):
        c = [coef[(at + k) & 7] for k in range(2)]
        keep = [1.0 - 4.0 * v for v in c]
        out = []
        for h in range(halves):
            w = [src[(at + k) & 3, h] for k in range(-1, 3)]
            for k in range(2):
                new = keep[k] * w[k + 1] + c[k] * ((w[k] + w[k + 2]) + around(w[k + 1]))
                if dst is None:
                    out.append(new)
                else:
                    dst[(at + k) & 3, h] = new
        return out

    def pair(p, _):
        i = step * ROWS + 2 * p
        rows = pl.ds(pl.multiple_of(i * PART, 2 * PART), 2 * PART)
        lhs = jnp.concatenate([stack[0, rows, :], stack[1, rows, :][:, :ext_y - 128]], axis=1).astype(BF16)
        wide = lax.dot_general(lhs, expand[...], TN, preferred_element_type=F32)
        for t in range(2 * width // 128):
            spread[t] = wide[:, 128 * t:128 * t + 128]
        gather = lambda t: jnp.stack([spread[t, pl.ds(v, 8, depth), :] for v in range(depth)])
        for k in range(2):
            at = i + k
            base = k * (width // 128)
            coef[at & 7] = gather(base + halves)
            back[at & 7] = gather(base + halves + 1)
            first_row, next_row = first[pl.ds(at, 1), :], first_next[pl.ds(at, 1), :]
            for h in range(halves):
                lanes = slice(128 * h, 128 * h + 128)
                scaled = gather(base + h)
                field[at & 7, h] = scaled
                probe = first_row[:, lanes][None] * second[h] + next_row[:, lanes][None] * second_next[h]
                w0[at & 3, h] = scaled * probe
        stencil(w0, i - 1, w1)
        stencil(w1, i - 2, w2)
        stencil(w2, i - 3, w3)
        last = stencil(w3, i - 4, None)
        for h in range(halves):
            for k in range(2):
                at = i - 4 + k
                value = field[at & 7, h] * (back[at & 7] * last[2 * h + k])
                for v in range(depth):
                    fold[2 * h + k, pl.ds(v, 8, depth), :] = value[v]
                lanes = slice(128 * h, 128 * h + 128)
                high_ref[2 * p + k, :, lanes], low_ref[2 * p + k, :, lanes] = split2(fold[2 * h + k, :ny])
        return 0

    lax.fori_loop(0, ROWS // 2, pair, 0)

    @pl.when(step > 0)
    def _():
        high = high_ref[...].reshape(ROWS * ny, dirs)
        low = low_ref[...].reshape(ROWS * ny, dirs)
        total[:, :dirs] += lax.dot_general(high, high, TN, preferred_element_type=F32)
        total[:, dirs:] += lax.dot_general(high, low, TN, preferred_element_type=F32)

    @pl.when(step == pl.num_programs(0) - 1)
    def _():
        cross = total[:, dirs:]
        total[:, :dirs] = total[:, :dirs] + cross + cross.T
        index = index_ref[0]
        strip = lambda at: total[pl.ds(pl.multiple_of(at * PROBES, PROBES), PROBES), :dirs]
        own_ref[...] = strip(index)
        other_ref[...] = strip(index ^ 1)


def responses(index, fields, stiffness, nx, ny):
    shots = fields.shape[0]
    dirs = shots * PROBES
    halves = dirs // 128
    ext_x, ext_y = nx + 2 * HALO, ny + 2 * HALO
    depth = ext_y // 8
    width = dirs + 256
    whole = lambda shape: pl.BlockSpec(shape, lambda s: (0,) * len(shape))
    block = pl.BlockSpec((ROWS, ny, dirs), lambda s: (jnp.maximum(s - 1, 0), 0, 0))
    return pl.pallas_call(
        functools.partial(response_kernel, shots, nx, ny),
        grid=(ext_x // ROWS,),
        in_specs=[SMEM, whole(fields.shape), whole(stiffness.shape)],
        out_specs=[whole((PROBES, dirs)), whole((PROBES, dirs)), block, block],
        out_shape=[
            jax.ShapeDtypeStruct((PROBES, dirs), F32),
            jax.ShapeDtypeStruct((PROBES, dirs), F32),
            jax.ShapeDtypeStruct((nx, ny, dirs), BF16),
            jax.ShapeDtypeStruct((nx, ny, dirs), BF16),
        ],
        scratch_shapes=[
            pltpu.VMEM((2 * PART, 2 * width), BF16),
            pltpu.VMEM((2, ext_x * PART, 128), F32),
            pltpu.VMEM((2 * width // 128, ext_y, 128), F32),
            pltpu.VMEM((ext_x, dirs), F32),
            pltpu.VMEM((ext_x, dirs), F32),
            pltpu.VMEM((halves, depth, 8, 128), F32),
            pltpu.VMEM((halves, depth, 8, 128), F32),
            pltpu.VMEM((8, depth, 8, 128), F32),
            pltpu.VMEM((8, depth, 8, 128), F32),
            pltpu.VMEM((8, halves, depth, 8, 128), F32),
            *[pltpu.VMEM((4, halves, depth, 8, 128), F32) for _ in range(4)],
            pltpu.VMEM((2 * halves, ext_y, 128), F32),
            pltpu.VMEM((dirs, 2 * dirs), F32),
        ],
        compiler_params=pltpu.CompilerParams(
            dimension_semantics=("arbitrary",), vmem_limit_bytes=48 * 2**20
        ),
        name="responses",
    )(index, fields, stiffness)


PANEL = 64
PIVOT = 4


def cholesky(n, gram_ref, table):
    tiles = n // 128
    eye_row = lax.broadcasted_iota(jnp.int32, (8, 128), 0)
    eye_col = lax.broadcasted_iota(jnp.int32, (8, 128), 1)
    table[:, :n] = gram_ref[...]
    full = lambda x: jnp.broadcast_to(x, (8, 128))
    for panel in range(n // PANEL):
        start = panel * PANEL
        tile = start // 128
        live = [*range(tile, tiles), *range(tiles, tiles + tile + 1)]
        rows = {}
        for g in range(PANEL // 8):
            for t in live:
                at = start + 8 * g
                value = None
                if t < tiles or panel > 0:
                    value = table[at:at + 8, 128 * t:128 * t + 128] if (t < tiles or (t - tiles) * 128 < start) else None
                if t >= tiles:
                    unit = (eye_row + at == eye_col + 128 * (t - tiles)).astype(F32)
                    value = unit if value is None else value + unit
                rows[g, t] = value
        for micro in range(PANEL // PIVOT):
            k = micro * PIVOT
            gp, r = k // 8, k % 8
            lane = (start + k) % 128
            pivot_rows = [{t: full(rows[gp, t][r + j:r + j + 1, :]) for t in live} for j in range(PIVOT)]
            a = {
                (i, j): full(pivot_rows[i][tile][:, lane + j:lane + j + 1])
                for i in range(PIVOT) for j in range(i + 1)
            }
            low, inv = {}, []
            for j in range(PIVOT):
                d = a[j, j]
                for m in range(j):
                    d = d - low[j, m] * low[j, m]
                inv.append(lax.rsqrt(d))
                for i in range(j + 1, PIVOT):
                    v = a[i, j]
                    for m in range(j):
                        v = v - low[i, m] * low[j, m]
                    low[i, j] = v * inv[j]
            ready = []
            for j in range(PIVOT):
                out = {}
                for t in live:
                    v = pivot_rows[j][t]
                    for m in range(j):
                        v = v - low[j, m] * ready[m][t]
                    out[t] = v * inv[j]
                ready.append(out)
            for g in range(gp, PANEL // 8):
                if g == gp and r + PIVOT == 8:
                    pass
                else:
                    cols = []
                    for j in range(PIVOT):
                        v = full(rows[g, tile][:, lane + j:lane + j + 1])
                        for m in range(j):
                            v = v - cols[m] * low[j, m]
                        cols.append(v * inv[j])
                    if g == gp:
                        cols = [jnp.where(eye_row >= r + PIVOT, v, 0.0) for v in cols]
                    for t in live:
                        v = rows[g, t]
                        for j in range(PIVOT):
                            v = v - cols[j] * ready[j][t]
                        rows[g, t] = v
                if g == gp:
                    for t in live:
                        v = rows[g, t]
                        for j in range(PIVOT):
                            v = jnp.where(eye_row == r + j, ready[j][t], v)
                        rows[g, t] = v
        for g in range(PANEL // 8):
            for t in live:
                at = start + 8 * g
                value = rows[g, t]
                if t == tile:
                    value = jnp.where(eye_row + at <= eye_col + 128 * t, value, 0.0)
                table[at:at + 8, 128 * t:128 * t + 128] = value
            for t in range(tile):
                table[start + 8 * g:start + 8 * g + 8, 128 * t:128 * t + 128] = jnp.zeros((8, 128), F32)
            for t in range(tiles + tile + 1, 2 * tiles):
                table[start + 8 * g:start + 8 * g + 8, 128 * t:128 * t + 128] = jnp.zeros((8, 128), F32)
        below = start + PANEL
        if below < n:
            keep = below // 128
            for t in range(keep, tiles + tile + 1):
                if t == keep:
                    lo = 128 * keep
                    left = table[start:below, lo:n]
                    p3 = [v.astype(BF16) for v in split3(left)]
                    lhs = jnp.concatenate([p3[0], p3[0], p3[1], p3[0], p3[2], p3[1]], axis=0)
                lanes = slice(128 * t, 128 * t + 128)
                right = [v.astype(BF16) for v in split3(table[start:below, lanes])]
                rhs = jnp.concatenate([right[0], right[1], right[0], right[2], right[0], right[1]], axis=0)
                update = lax.dot_general(lhs, rhs, TN, preferred_element_type=F32)[below - lo:]
                if t < tiles or 128 * (t - tiles) < start:
                    table[below:, lanes] = table[below:, lanes] - update
                else:
                    table[below:, lanes] = -update

def finish_kernel(n, scale, index_ref, gram_ref, high_hbm, low_hbm, upper_ref, own_ref, other_ref,
                  table, high_ref, low_ref, sems):
    copies = [
        pltpu.make_async_copy(high_hbm, high_ref, sems.at[0]),
        pltpu.make_async_copy(low_hbm, low_ref, sems.at[1]),
    ]
    for copy in copies:
        copy.start()
    cholesky(n, gram_ref, table)
    index = index_ref[0]
    strip = lambda at: pl.ds(pl.multiple_of(at * PROBES, PROBES), PROBES)
    upper_ref[...] = table[strip(index), :n] * (1.0 / scale)
    rows = jnp.concatenate([table[strip(index), n:], table[strip(index ^ 1), n:]], axis=0) * scale
    high, low = split2(rows)
    both = jnp.concatenate([high, low], axis=0)
    for copy in copies:
        copy.wait()
    count, ny = high_ref.shape[:2]
    for i in range(0, count, 2):
        main = lax.dot_general(both, high_ref[i:i + 2].reshape(2 * ny, n), NT, preferred_element_type=F32)
        rest = lax.dot_general(high, low_ref[i:i + 2].reshape(2 * ny, n), NT, preferred_element_type=F32)
        value = main[:2 * PROBES] + (main[2 * PROBES:] + rest)
        for k in range(2):
            own_ref[:, i + k, :] = value[:PROBES, ny * k:ny * k + ny]
            other_ref[:, i + k, :] = value[PROBES:, ny * k:ny * k + ny]


def finish(index, gram, high, low, scale):
    n = gram.shape[0]
    nx, ny = high.shape[:2]
    return pl.pallas_call(
        functools.partial(finish_kernel, n, scale),
        in_specs=[SMEM, VMEM, HBM, HBM],
        out_specs=[VMEM] * 3,
        out_shape=[
            jax.ShapeDtypeStruct((PROBES, n), F32),
            jax.ShapeDtypeStruct((PROBES, nx, ny), F32),
            jax.ShapeDtypeStruct((PROBES, nx, ny), F32),
        ],
        scratch_shapes=[
            pltpu.VMEM((n, 2 * n), F32),
            pltpu.VMEM(high.shape, BF16),
            pltpu.VMEM(low.shape, BF16),
            pltpu.SemaphoreType.DMA((2,)),
        ],
        compiler_params=pltpu.CompilerParams(vmem_limit_bytes=48 * 2**20),
        name="finish",
    )(index, gram, high, low)


def shards(signs_x, signs_y, heights, velocity, background):
    shots = lax.axis_size("dir")
    nx, ny = background.shape[1:]
    ext_x, ext_y = nx + 2 * HALO, ny + 2 * HALO
    half = nx // 2
    index = lax.axis_index("dir")
    which = index.reshape(1)
    stiffness, first, last = small(
        pack_x_kernel, [(nx, ny), (16, ny), (16, ny)], [VMEM] * 4, "pack_x"
    )(signs_x, heights, velocity, background)
    above, below = exchange(first, last, "sx")
    field, stiffness, octets, first, last = small(
        pack_y_kernel, [(ext_x, ny), (ext_x, ny), (8, ny), (ext_x + 8, ny), (ext_x + 8, ny)], [VMEM] * 6, "pack_y"
    )(signs_y, background, stiffness, first, above, below)
    left, right = exchange(first, last, "sy")
    send, stiffness = small(
        pack_dir_kernel, [(shots, half + 2 * HALO + 8, ext_y), (half + 2 * HALO, ext_y)], [SMEM] + [VMEM] * 6, "pack_dir"
    )(which, field, stiffness, octets, first, left, right)
    fields = lax.all_to_all(send, "dir", 0, 0)
    own, other, high, low = responses(which, fields, stiffness, half, ny)
    swap = [(i, i ^ 1) for i in range(shots)]
    dirs = shots * PROBES
    strip = own + lax.ppermute(other, "dir", swap)
    terms = lax.all_to_all(strip.reshape(PROBES, dirs // 128, 128), ("sx", "sy"), 0, 0)
    row = jnp.sum(terms, axis=0, keepdims=True)
    gram = lax.all_to_all(jnp.broadcast_to(row, (dirs, *row.shape[1:])), ("dir", "sx", "sy"), 0, 0)
    gram = gram.reshape(dirs, dirs)
    scale = math.sqrt(nx * ny * lax.axis_size("sx") * lax.axis_size("sy"))
    factor, own, other = finish(which, gram, high, low, scale)
    other = lax.ppermute(other, "dir", swap)
    upper = index & 1 == 1
    basis = jnp.concatenate([jnp.where(upper, other, own), jnp.where(upper, own, other)], axis=1)
    return basis, factor


def solution(mesh):
    in_specs = (P("dir", "sx"), P("dir", "sy"), P("sx", "sy"), P("sx", "sy"), P("dir", "sx", "sy"))
    out_specs = (P("dir", "sx", "sy"), P("dir", None))
    return jax.shard_map(shards, mesh=mesh, in_specs=in_specs, out_specs=out_specs, check_vma=False)
```

```python
import functools
import math

import jax
import jax.numpy as jnp
from jax import lax
from jax.experimental import pallas as pl
from jax.experimental.pallas import tpu as pltpu
from jax.sharding import PartitionSpec as P

PROBES = 32
LEVELS = 64
HALO = 4
ROWS = 8
tau_step = 0.02

F32 = jnp.float32
BF16 = jnp.bfloat16
TN = (((0,), (0,)), ((), ()))
NT = (((1,), (1,)), ((), ()))
VMEM = pl.BlockSpec(memory_space=pltpu.VMEM)
SMEM = pl.BlockSpec(memory_space=pltpu.SMEM)


def split2(x):
    high = x.astype(BF16)
    return high, (x - high.astype(F32)).astype(BF16)


def split3(x):
    high = x.astype(BF16).astype(F32)
    rest = x - high
    mid = rest.astype(BF16).astype(F32)
    return high, mid, rest - mid


def sign_bytes(words):
    shape = (8, words.shape[1])
    shift = 8 * (lax.broadcasted_iota(jnp.int32, shape, 0) & 3)
    return (jnp.right_shift(jnp.broadcast_to(words, shape), shift) & 255).astype(F32)


def pack_x_kernel(signs_ref, heights_ref, velocity_ref, field_ref, stiff_ref, first_ref, last_ref):
    nx, ny = velocity_ref.shape
    stiff = velocity_ref[...] * jnp.sqrt(1.0 + heights_ref[...].astype(F32) / LEVELS)
    stiff_ref[...] = stiff
    octets = sign_bytes(signs_ref[...])
    for ref, start in ((first_ref, 0), (last_ref, nx - HALO)):
        ref[0:HALO, :] = field_ref[0, start:start + HALO, :]
        ref[HALO:2 * HALO, :] = stiff[start:start + HALO]
        ref[8:16, :] = jnp.zeros((8, ny), F32)
        ref[8:16, :nx] = octets


def pack_y_kernel(signs_ref, field_ref, stiff_ref, own_ref, above_ref, below_ref,
                  field_out, stiff_out, octets_out, first_ref, last_ref):
    nx, ny = stiff_ref.shape
    ext_x = nx + 2 * HALO
    field_out[0:HALO, :] = above_ref[0:HALO, :]
    field_out[HALO:HALO + nx, :] = field_ref[0]
    field_out[HALO + nx:ext_x, :] = below_ref[0:HALO, :]
    stiff_out[0:HALO, :] = above_ref[HALO:2 * HALO, :]
    stiff_out[HALO:HALO + nx, :] = stiff_ref[...]
    stiff_out[HALO + nx:ext_x, :] = below_ref[HALO:2 * HALO, :]
    lane = lax.broadcasted_iota(jnp.int32, (8, ny), 1)
    after = pltpu.roll(below_ref[8:16, :], nx + HALO, 1)
    before = pltpu.roll(above_ref[8:16, :], ny - nx + HALO, 1)
    own = pltpu.roll(own_ref[8:16, :], HALO, 1)
    octets_out[...] = jnp.where(lane < HALO, before, jnp.where(lane < HALO + nx, own, after))
    octets = sign_bytes(signs_ref[...])
    field, stiff = field_out[...], stiff_out[...]
    lane = lax.broadcasted_iota(jnp.int32, field.shape, 1)
    first_ref[0:ext_x, :] = jnp.where(lane < HALO, field, pltpu.roll(stiff, HALO, 1))
    first_ref[ext_x:, :] = octets
    last_ref[0:ext_x, :] = jnp.where(lane < 2 * HALO, pltpu.roll(field, 2 * HALO, 1), pltpu.roll(stiff, 3 * HALO, 1))
    last_ref[ext_x:, :] = octets


def pack_dir_kernel(index_ref, field_ref, stiff_ref, octets_ref, own_ref, left_ref, right_ref, send_ref, stiff_out):
    ext_x, ny = field_ref.shape
    half = (ext_x - 2 * HALO) // 2
    take = half + 2 * HALO
    left, right = left_ref[0:ext_x, :], right_ref[0:ext_x, :]
    lane = lax.broadcasted_iota(jnp.int32, left.shape, 1)
    field_side = jnp.where(lane < HALO, right, left)
    shift = lambda v: pltpu.roll(v, ny - HALO, 1)
    stiff_side = jnp.where(lane < HALO, shift(right), shift(left))
    lane = lax.broadcasted_iota(jnp.int32, (8, ny), 1)
    octet_side = jnp.where(lane < HALO, right_ref[ext_x:, :], pltpu.roll(left_ref[ext_x:, :], 2 * HALO, 1))
    own_octets = own_ref[ext_x:, :]
    for dest in range(send_ref.shape[0]):
        part = dest & 1
        rows = slice(part * half, part * half + take)
        send_ref[dest, 0:take, 0:ny] = field_ref[rows, :]
        send_ref[dest, 0:take, ny:] = field_side[rows, :2 * HALO]
        x_octets = octets_ref[...] if part == 0 else pltpu.roll(octets_ref[...], ny - half, 1)
        send_ref[dest, take:take + 4, 0:ny] = x_octets[0:4]
        send_ref[dest, take:take + 4, ny:] = jnp.zeros((4, 2 * HALO), F32)
        send_ref[dest, take + 4:take + 8, 0:ny] = own_octets[0:4]
        send_ref[dest, take + 4:take + 8, ny:] = octet_side[0:4, :2 * HALO]
    row = pl.multiple_of((index_ref[0] & 1) * half, half)
    stiff_out[:, 0:ny] = stiff_ref[pl.ds(row, take), :]
    spare = jnp.where(index_ref[0] & 1 == 1, stiff_side[half:half + take], stiff_side[0:take])
    stiff_out[:, ny:] = spare[:, :2 * HALO]


def small(kernel, shapes, specs, name):
    return pl.pallas_call(
        kernel,
        in_specs=specs,
        out_specs=[VMEM] * len(shapes),
        out_shape=[jax.ShapeDtypeStruct(shape, F32) for shape in shapes],
        compiler_params=pltpu.CompilerParams(vmem_limit_bytes=4 * 2**20),
        name=name,
    )


def exchange(first, last, axis):
    count = lax.axis_size(axis)
    before = lax.ppermute(last, axis, [(i, i + 1) for i in range(count - 1)])
    after = lax.ppermute(first, axis, [(i + 1, i) for i in range(count - 1)])
    return before, after


PART = 32


def response_kernel(shots, nx, ny, index_ref, field_ref, stiff_ref, own_ref, other_ref, parts_ref,
                    expand, stack, spread, first, first_next, second, second_next,
                    w0, w1, w2, w3, fold, total):
    dirs = shots * PROBES
    halves = dirs // 128
    ext_x, ext_y = nx + 2 * HALO, ny + 2 * HALO
    depth = ny // 8
    width = dirs + 256
    step = pl.program_id(0)
    sub = lax.broadcasted_iota(jnp.int32, (8, 128), 0)

    def at_cell(slot, t, v):
        return spread[slot, t, pl.ds(v, 8, depth), :] if v < depth else spread[slot, t, ny:ext_y, :]

    def widen(i, slot):
        rows = pl.ds(pl.multiple_of(i * PART, 2 * PART), 2 * PART)
        lhs = jnp.concatenate([stack[0, rows, :], stack[1, rows, :][:, :ext_y - 128]], axis=1).astype(BF16)
        wide = lax.dot_general(lhs, expand[...], TN, preferred_element_type=F32)
        for t in range(2 * width // 128):
            spread[slot, t] = wide[:, 128 * t:128 * t + 128]

    @pl.when(step == 0)
    def _():
        total[...] = jnp.zeros_like(total)
        row = lax.broadcasted_iota(jnp.int32, (2 * PART, 2 * width), 0)
        col = lax.broadcasted_iota(jnp.int32, (2 * PART, 2 * width), 1)
        same = row // PART == col // width
        row, col = row % PART, col % width
        pick = (row < 24) & (row % 8 == col // PROBES) & (col < dirs)
        pick |= (row >= 24) & (row < 27) & (col >= dirs) & (col < dirs + 128)
        pick |= (row >= 27) & (row < 30) & (col >= dirs + 128)
        expand[...] = jnp.where(pick & same, 1.0, 0.0).astype(BF16)
        s = stiff_ref[...]
        stack[...] = jnp.zeros_like(stack)

        def put(value, at):
            where = pl.ds(at, ext_x, PART)
            stack[0, where, :] = value[:, :128]
            stack[1, where, :] = jnp.concatenate([value[:, 128:], jnp.zeros((ext_x, 256 - ext_y), F32)], axis=1)

        for g in range(shots):
            for part, value in enumerate(split3(field_ref[g, :ext_x, :] * s)):
                put(value, 8 * part + g)
        square = s * s
        for part, value in enumerate(split3(tau_step * square)):
            put(value, 24 + part)
        for part, value in enumerate(split3(1.0 / jnp.where(s > 0.0, square, 1.0))):
            put(value, 27 + part)
        words = jnp.concatenate(
            [field_ref[g, ext_x:ext_x + 8, :] for g in range(shots)], axis=0
        ).astype(BF16)
        row = lax.broadcasted_iota(jnp.int32, (8 * shots, dirs), 0)
        col = lax.broadcasted_iota(jnp.int32, (8 * shots, dirs), 1)

        def bits(offset, shift):
            probe = (col + shift) % PROBES
            hit = (row // 8 == col // PROBES) & (row % 8 - offset == probe // 8)
            value = lax.dot_general(words, jnp.where(hit, 1.0, 0.0).astype(BF16), TN, preferred_element_type=F32)
            lane = (lax.broadcasted_iota(jnp.int32, value.shape, 1) + shift) % 8
            bit = jnp.right_shift(value.astype(jnp.int32), lane) & 1
            return (2 * bit - 1).astype(F32)

        first[...] = bits(0, 0)[:ext_x]
        first_next[...] = 0.5 * bits(0, 1)[:ext_x]
        for ref, shift in ((second, 0), (second_next, 1)):
            value = bits(4, shift)
            for h in range(halves):
                spread[0, h] = value[:, 128 * h:128 * h + 128]
                for v in range(depth + 1):
                    ref[h, v] = at_cell(0, h, v)
        widen(0, 0)

    pairs = ROWS // 2
    count = width // 128

    def place(row):
        return (row >> 1) & (pairs - 1), (row & 1) * count

    def stencil(src, at, emit):
        centre, upper, lower, edge = {}, {}, {}, {}
        for h in range(halves):
            for k in range(2):
                ref = src.at[(at + k) & 3, h]
                head, tail, halo = ref[0], ref[depth - 1], ref[depth]
                head_up, halo_up = pltpu.roll(head, 7, 0), pltpu.roll(halo, 7, 0)
                tail_down, halo_down = pltpu.roll(tail, 1, 0), pltpu.roll(halo, 1, 0)
                edge[h, k] = jnp.where(sub == 7, halo_up, head_up)
                after_halo = jnp.where(sub == 7, head_up, halo_up)
                before_head = jnp.where(sub == 0, halo_down, tail_down)
                before_halo = jnp.where(sub == 0, tail_down, halo_down)
                lower[h, k], centre[h, k] = before_head, head
                upper[h, k] = after_halo + before_halo
        for v in range(depth + 1):
            c = [at_cell(*[place(at + k)[0], place(at + k)[1] + halves], v) for k in range(2)]
            for h in range(halves):
                above = src[(at - 1) & 3, h, v]
                below = src[(at + 2) & 3, h, v]
                if v == depth:
                    for k in range(2):
                        centre[h, k] = src[(at + k) & 3, h, v]
                mid = [centre[h, k] for k in range(2)]
                for k in range(2):
                    if v < depth:
                        after = src[(at + k) & 3, h, v + 1] if v < depth - 1 else edge[h, k]
                        side = after + lower[h, k]
                        lower[h, k], centre[h, k] = mid[k], after
                    else:
                        side = upper[h, k]
                    beside = (above + mid[1]) if k == 0 else (mid[0] + below)
                    emit(k, h, v, mid[k] + c[k] * ((beside + side) - 4.0 * mid[k]))

    def level(src, at, dst):
        def emit(k, h, v, value):
            dst[(at + k) & 3, h, v] = value
        stencil(src, at, emit)

    for p in range(pairs):
        i = 2 * p
        first_row = [first[pl.ds(step * ROWS + i + k, 1), :] for k in range(2)]
        next_row = [first_next[pl.ds(step * ROWS + i + k, 1), :] for k in range(2)]
        for v in range(depth + 1):
            for h in range(halves):
                lanes = slice(128 * h, 128 * h + 128)
                one, two = second[h, v], second_next[h, v]
                for k in range(2):
                    probe = first_row[k][:, lanes] * one + next_row[k][:, lanes] * two
                    slot, tile = place(i + k)
                    w0[(i + k) & 3, h, v] = at_cell(slot, tile + h, v) * probe
        widen(jnp.minimum(step * ROWS + i + 2, ext_x - 2), (p + 1) % pairs)
        level(w0, i - 1, w1)
        level(w1, i - 2, w2)
        level(w2, i - 3, w3)

        def emit(k, h, v, value):
            if v < depth:
                slot, tile = place(i - 4 + k)
                scale = at_cell(slot, tile + h, v) * at_cell(slot, tile + halves + 1, v)
                fold[2 * h + k, 8 * v:8 * v + 8, :] = scale * value

        stencil(w3, i - 4, emit)
        for h in range(halves):
            for k in range(2):
                for q in range(0, depth, 2):
                    value = jnp.concatenate(
                        [fold[2 * h + k, pl.ds(8 * (r % depth) + r // depth, 8, 8), :] for r in (8 * q, 8 * q + 8)], axis=0
                    )
                    for part, piece in enumerate(split2(value)):
                        at_lane = part * dirs + 128 * h
                        parts_ref[i + k, 8 * q:8 * q + 16, at_lane:at_lane + 128] = piece

    @pl.when(step > 0)
    def _():
        parts = parts_ref[...].reshape(ROWS * ny, 2 * dirs)
        total[...] += lax.dot_general(parts[:, :dirs], parts, TN, preferred_element_type=F32)

    @pl.when(step == pl.num_programs(0) - 1)
    def _():
        cross = total[:, dirs:]
        total[:, :dirs] = total[:, :dirs] + cross + cross.T
        index = index_ref[0]
        strip = lambda at: total[pl.ds(pl.multiple_of(at * PROBES, PROBES), PROBES), :dirs]
        own_ref[...] = strip(index)
        other_ref[...] = strip(index ^ 1)


def responses(index, fields, stiffness, nx, ny):
    shots = fields.shape[0]
    dirs = shots * PROBES
    halves = dirs // 128
    ext_x, ext_y = nx + 2 * HALO, ny + 2 * HALO
    blocks = ext_y // 8
    width = dirs + 256
    whole = lambda shape: pl.BlockSpec(shape, lambda s: (0,) * len(shape))
    block = pl.BlockSpec((ROWS, ny, 2 * dirs), lambda s: (jnp.maximum(s - 1, 0), 0, 0))
    return pl.pallas_call(
        functools.partial(response_kernel, shots, nx, ny),
        grid=(ext_x // ROWS,),
        in_specs=[SMEM, whole(fields.shape), whole(stiffness.shape)],
        out_specs=[whole((PROBES, dirs)), whole((PROBES, dirs)), block],
        out_shape=[
            jax.ShapeDtypeStruct((PROBES, dirs), F32),
            jax.ShapeDtypeStruct((PROBES, dirs), F32),
            jax.ShapeDtypeStruct((nx, ny, 2 * dirs), BF16),
        ],
        scratch_shapes=[
            pltpu.VMEM((2 * PART, 2 * width), BF16),
            pltpu.VMEM((2, ext_x * PART, 128), F32),
            pltpu.VMEM((ROWS // 2, 2 * width // 128, ext_y, 128), F32),
            pltpu.VMEM((ext_x, dirs), F32),
            pltpu.VMEM((ext_x, dirs), F32),
            pltpu.VMEM((halves, blocks, 8, 128), F32),
            pltpu.VMEM((halves, blocks, 8, 128), F32),
            *[pltpu.VMEM((4, halves, blocks, 8, 128), F32) for _ in range(4)],
            pltpu.VMEM((2 * halves, ny, 128), F32),
            pltpu.VMEM((dirs, 2 * dirs), F32),
        ],
        compiler_params=pltpu.CompilerParams(
            dimension_semantics=("arbitrary",), vmem_limit_bytes=61 * 2**20
        ),
        name="responses",
    )(index, fields, stiffness)


PANEL = 64
PIVOT = 8


def cholesky(n, gram_ref, table):
    tiles = n // 128
    eye_row = lax.broadcasted_iota(jnp.int32, (8, 128), 0)
    eye_col = lax.broadcasted_iota(jnp.int32, (8, 128), 1)
    table[:, :n] = gram_ref[...]
    full = lambda x: jnp.broadcast_to(x, (8, 128))
    for panel in range(n // PANEL):
        start = panel * PANEL
        tile = start // 128
        live = [*range(tile, tiles), *range(tiles, tiles + tile + 1)]
        rows = {}
        for g in range(PANEL // 8):
            for t in live:
                at = start + 8 * g
                value = None
                if t < tiles or panel > 0:
                    value = table[at:at + 8, 128 * t:128 * t + 128] if (t < tiles or (t - tiles) * 128 < start) else None
                if t >= tiles:
                    unit = (eye_row + at == eye_col + 128 * (t - tiles)).astype(F32)
                    value = unit if value is None else value + unit
                rows[g, t] = value
        for micro in range(PANEL // PIVOT):
            k = micro * PIVOT
            gp, r = k // 8, k % 8
            lane = (start + k) % 128
            pivot_rows = [{t: full(rows[gp, t][r + j:r + j + 1, :]) for t in live} for j in range(PIVOT)]
            a = {
                (i, j): full(pivot_rows[i][tile][:, lane + j:lane + j + 1])
                for i in range(PIVOT) for j in range(i + 1)
            }
            low, inv = {}, []
            for j in range(PIVOT):
                d = a[j, j]
                for m in range(j):
                    d = d - low[j, m] * low[j, m]
                inv.append(lax.rsqrt(d))
                for i in range(j + 1, PIVOT):
                    v = a[i, j]
                    for m in range(j):
                        v = v - low[i, m] * low[j, m]
                    low[i, j] = v * inv[j]
            ready = []
            for j in range(PIVOT):
                out = {}
                for t in live:
                    v = pivot_rows[j][t]
                    for m in range(j):
                        v = v - low[j, m] * ready[m][t]
                    out[t] = v * inv[j]
                ready.append(out)
            for g in range(gp, PANEL // 8):
                if g == gp and r + PIVOT == 8:
                    pass
                else:
                    cols = []
                    for j in range(PIVOT):
                        v = full(rows[g, tile][:, lane + j:lane + j + 1])
                        for m in range(j):
                            v = v - cols[m] * low[j, m]
                        cols.append(v * inv[j])
                    if g == gp:
                        cols = [jnp.where(eye_row >= r + PIVOT, v, 0.0) for v in cols]
                    for t in live:
                        v = rows[g, t]
                        for j in range(PIVOT):
                            v = v - cols[j] * ready[j][t]
                        rows[g, t] = v
                if g == gp:
                    for t in live:
                        v = rows[g, t]
                        for j in range(PIVOT):
                            v = jnp.where(eye_row == r + j, ready[j][t], v)
                        rows[g, t] = v
        for g in range(PANEL // 8):
            for t in live:
                at = start + 8 * g
                value = rows[g, t]
                if t == tile:
                    value = jnp.where(eye_row + at <= eye_col + 128 * t, value, 0.0)
                table[at:at + 8, 128 * t:128 * t + 128] = value
            for t in range(tile):
                table[start + 8 * g:start + 8 * g + 8, 128 * t:128 * t + 128] = jnp.zeros((8, 128), F32)
            for t in range(tiles + tile + 1, 2 * tiles):
                table[start + 8 * g:start + 8 * g + 8, 128 * t:128 * t + 128] = jnp.zeros((8, 128), F32)
        below = start + PANEL
        if below < n:
            keep = below // 128
            for t in range(keep, tiles + tile + 1):
                if t == keep:
                    lo = 128 * keep
                    left = table[start:below, lo:n]
                    p3 = [v.astype(BF16) for v in split3(left)]
                    lhs = jnp.concatenate([p3[0], p3[0], p3[1], p3[0], p3[2], p3[1]], axis=0)
                lanes = slice(128 * t, 128 * t + 128)
                right = [v.astype(BF16) for v in split3(table[start:below, lanes])]
                rhs = jnp.concatenate([right[0], right[1], right[0], right[2], right[0], right[1]], axis=0)
                update = lax.dot_general(lhs, rhs, TN, preferred_element_type=F32)[below - lo:]
                if t < tiles or 128 * (t - tiles) < start:
                    table[below:, lanes] = table[below:, lanes] - update
                else:
                    table[below:, lanes] = -update

def finish_kernel(n, scale, index_ref, gram_ref, parts_any, upper_ref, own_ref, other_ref, table, parts_ref, sem):
    copy = pltpu.make_async_copy(parts_any, parts_ref, sem)
    copy.start()
    cholesky(n, gram_ref, table)
    index = index_ref[0]
    strip = lambda at: pl.ds(pl.multiple_of(at * PROBES, PROBES), PROBES)
    upper_ref[...] = table[strip(index), :n] * (1.0 / scale)
    rows = jnp.concatenate([table[strip(index), n:], table[strip(index ^ 1), n:]], axis=0) * scale
    high, low = split2(rows)
    both = jnp.concatenate([high, low], axis=0)
    copy.wait()
    count, ny = parts_ref.shape[:2]
    for i in range(0, count, 2):
        parts = parts_ref[i:i + 2].reshape(2 * ny, 2 * n)
        main = lax.dot_general(both, parts[:, :n], NT, preferred_element_type=F32)
        rest = lax.dot_general(high, parts[:, n:], NT, preferred_element_type=F32)
        value = main[:2 * PROBES] + (main[2 * PROBES:] + rest)
        for k in range(2):
            own_ref[:, i + k, :] = value[:PROBES, ny * k:ny * k + ny]
            other_ref[:, i + k, :] = value[PROBES:, ny * k:ny * k + ny]


def finish(index, gram, parts, scale):
    n = gram.shape[0]
    nx, ny = parts.shape[:2]
    return pl.pallas_call(
        functools.partial(finish_kernel, n, scale),
        in_specs=[SMEM, VMEM, pl.BlockSpec(memory_space=pl.ANY)],
        out_specs=[VMEM] * 3,
        out_shape=[
            jax.ShapeDtypeStruct((PROBES, n), F32),
            jax.ShapeDtypeStruct((PROBES, nx, ny), F32),
            jax.ShapeDtypeStruct((PROBES, nx, ny), F32),
        ],
        scratch_shapes=[
            pltpu.VMEM((n, 2 * n), F32),
            pltpu.VMEM(parts.shape, BF16),
            pltpu.SemaphoreType.DMA,
        ],
        compiler_params=pltpu.CompilerParams(vmem_limit_bytes=61 * 2**20),
        name="finish",
    )(index, gram, parts)


def shards(signs_x, signs_y, heights, velocity, background):
    shots = lax.axis_size("dir")
    nx, ny = background.shape[1:]
    ext_x, ext_y = nx + 2 * HALO, ny + 2 * HALO
    half = nx // 2
    index = lax.axis_index("dir")
    which = index.reshape(1)
    stiffness, first, last = small(
        pack_x_kernel, [(nx, ny), (16, ny), (16, ny)], [VMEM] * 4, "pack_x"
    )(signs_x, heights, velocity, background)
    above, below = exchange(first, last, "sx")
    field, stiffness, octets, first, last = small(
        pack_y_kernel, [(ext_x, ny), (ext_x, ny), (8, ny), (ext_x + 8, ny), (ext_x + 8, ny)], [VMEM] * 6, "pack_y"
    )(signs_y, background, stiffness, first, above, below)
    left, right = exchange(first, last, "sy")
    send, stiffness = small(
        pack_dir_kernel, [(shots, half + 2 * HALO + 8, ext_y), (half + 2 * HALO, ext_y)], [SMEM] + [VMEM] * 6, "pack_dir"
    )(which, field, stiffness, octets, first, left, right)
    fields = lax.all_to_all(send, "dir", 0, 0)
    own, other, parts = responses(which, fields, stiffness, half, ny)
    swap = [(i, i ^ 1) for i in range(shots)]
    dirs = shots * PROBES
    strip = own + lax.ppermute(other, "dir", swap)
    terms = lax.all_to_all(strip.reshape(PROBES, dirs // 128, 128), ("sx", "sy"), 0, 0)
    row = jnp.sum(terms, axis=0, keepdims=True)
    gram = lax.all_to_all(jnp.broadcast_to(row, (dirs, *row.shape[1:])), ("dir", "sx", "sy"), 0, 0)
    gram = gram.reshape(dirs, dirs)
    scale = math.sqrt(nx * ny * lax.axis_size("sx") * lax.axis_size("sy"))
    factor, own, other = finish(which, gram, parts, scale)
    other = lax.ppermute(other, "dir", swap)
    upper = index & 1 == 1
    basis = jnp.concatenate([jnp.where(upper, other, own), jnp.where(upper, own, other)], axis=1)
    return basis, factor


def solution(mesh):
    in_specs = (P("dir", "sx"), P("dir", "sy"), P("sx", "sy"), P("sx", "sy"), P("dir", "sx", "sy"))
    out_specs = (P("dir", "sx", "sy"), P("dir", None))
    return jax.shard_map(shards, mesh=mesh, in_specs=in_specs, out_specs=out_specs, check_vma=False)
```

```python
import functools
import math

import jax
import jax.numpy as jnp
from jax import lax
from jax.experimental import pallas as pl
from jax.experimental.pallas import tpu as pltpu
from jax.sharding import PartitionSpec as P

PROBES = 32
LEVELS = 64
HALO = 4
ROWS = 8
tau_step = 0.02

F32 = jnp.float32
BF16 = jnp.bfloat16
TN = (((0,), (0,)), ((), ()))
NT = (((1,), (1,)), ((), ()))
VMEM = pl.BlockSpec(memory_space=pltpu.VMEM)
SMEM = pl.BlockSpec(memory_space=pltpu.SMEM)


def split2(x):
    high = x.astype(BF16)
    return high, (x - high.astype(F32)).astype(BF16)


def split3(x):
    high = x.astype(BF16).astype(F32)
    rest = x - high
    mid = rest.astype(BF16).astype(F32)
    return high, mid, rest - mid


def sign_bytes(words):
    shape = (8, words.shape[1])
    shift = 8 * (lax.broadcasted_iota(jnp.int32, shape, 0) & 3)
    return (jnp.right_shift(jnp.broadcast_to(words, shape), shift) & 255).astype(F32)


def pack_x_kernel(signs_ref, heights_ref, velocity_ref, field_ref, stiff_ref, first_ref, last_ref):
    nx, ny = velocity_ref.shape
    stiff = velocity_ref[...] * jnp.sqrt(1.0 + heights_ref[...].astype(F32) / LEVELS)
    stiff_ref[...] = stiff
    octets = sign_bytes(signs_ref[...])
    for ref, start in ((first_ref, 0), (last_ref, nx - HALO)):
        ref[0:HALO, :] = field_ref[0, start:start + HALO, :]
        ref[HALO:2 * HALO, :] = stiff[start:start + HALO]
        ref[8:16, :] = jnp.zeros((8, ny), F32)
        ref[8:16, :nx] = octets


def pack_y_kernel(signs_ref, field_ref, stiff_ref, own_ref, above_ref, below_ref,
                  field_out, stiff_out, octets_out, first_ref, last_ref):
    nx, ny = stiff_ref.shape
    ext_x = nx + 2 * HALO
    field_out[0:HALO, :] = above_ref[0:HALO, :]
    field_out[HALO:HALO + nx, :] = field_ref[0]
    field_out[HALO + nx:ext_x, :] = below_ref[0:HALO, :]
    stiff_out[0:HALO, :] = above_ref[HALO:2 * HALO, :]
    stiff_out[HALO:HALO + nx, :] = stiff_ref[...]
    stiff_out[HALO + nx:ext_x, :] = below_ref[HALO:2 * HALO, :]
    lane = lax.broadcasted_iota(jnp.int32, (8, ny), 1)
    after = pltpu.roll(below_ref[8:16, :], nx + HALO, 1)
    before = pltpu.roll(above_ref[8:16, :], ny - nx + HALO, 1)
    own = pltpu.roll(own_ref[8:16, :], HALO, 1)
    octets_out[...] = jnp.where(lane < HALO, before, jnp.where(lane < HALO + nx, own, after))
    octets = sign_bytes(signs_ref[...])
    field, stiff = field_out[...], stiff_out[...]
    lane = lax.broadcasted_iota(jnp.int32, field.shape, 1)
    first_ref[0:ext_x, :] = jnp.where(lane < HALO, field, pltpu.roll(stiff, HALO, 1))
    first_ref[ext_x:, :] = octets
    last_ref[0:ext_x, :] = jnp.where(lane < 2 * HALO, pltpu.roll(field, 2 * HALO, 1), pltpu.roll(stiff, 3 * HALO, 1))
    last_ref[ext_x:, :] = octets


def pack_dir_kernel(index_ref, field_ref, stiff_ref, octets_ref, own_ref, left_ref, right_ref, send_ref, stiff_out):
    ext_x, ny = field_ref.shape
    half = (ext_x - 2 * HALO) // 2
    take = half + 2 * HALO
    left, right = left_ref[0:ext_x, :], right_ref[0:ext_x, :]
    lane = lax.broadcasted_iota(jnp.int32, left.shape, 1)
    field_side = jnp.where(lane < HALO, right, left)
    shift = lambda v: pltpu.roll(v, ny - HALO, 1)
    stiff_side = jnp.where(lane < HALO, shift(right), shift(left))
    lane = lax.broadcasted_iota(jnp.int32, (8, ny), 1)
    octet_side = jnp.where(lane < HALO, right_ref[ext_x:, :], pltpu.roll(left_ref[ext_x:, :], 2 * HALO, 1))
    own_octets = own_ref[ext_x:, :]
    for dest in range(send_ref.shape[0]):
        part = dest & 1
        rows = slice(part * half, part * half + take)
        send_ref[dest, 0:take, 0:ny] = field_ref[rows, :]
        send_ref[dest, 0:take, ny:] = field_side[rows, :2 * HALO]
        x_octets = octets_ref[...] if part == 0 else pltpu.roll(octets_ref[...], ny - half, 1)
        send_ref[dest, take:take + 4, 0:ny] = x_octets[0:4]
        send_ref[dest, take:take + 4, ny:] = jnp.zeros((4, 2 * HALO), F32)
        send_ref[dest, take + 4:take + 8, 0:ny] = own_octets[0:4]
        send_ref[dest, take + 4:take + 8, ny:] = octet_side[0:4, :2 * HALO]
    row = pl.multiple_of((index_ref[0] & 1) * half, half)
    stiff_out[:, 0:ny] = stiff_ref[pl.ds(row, take), :]
    spare = jnp.where(index_ref[0] & 1 == 1, stiff_side[half:half + take], stiff_side[0:take])
    stiff_out[:, ny:] = spare[:, :2 * HALO]


def small(kernel, shapes, specs, name, limit=4):
    return pl.pallas_call(
        kernel,
        in_specs=specs,
        out_specs=[VMEM] * len(shapes),
        out_shape=[jax.ShapeDtypeStruct(shape, F32) for shape in shapes],
        compiler_params=pltpu.CompilerParams(vmem_limit_bytes=limit * 2**20),
        name=name,
    )


def exchange(first, last, axis):
    count = lax.axis_size(axis)
    before = lax.ppermute(last, axis, [(i, i + 1) for i in range(count - 1)])
    after = lax.ppermute(first, axis, [(i + 1, i) for i in range(count - 1)])
    return before, after


PART = 32


def response_kernel(shots, nx, ny, index_ref, field_ref, stiff_ref, own_ref, other_ref, parts_ref,
                    expand, stack, spread, first, first_next, second, second_next,
                    w0, w1, w2, w3, fold, total):
    dirs = shots * PROBES
    halves = dirs // 128
    ext_x, ext_y = nx + 2 * HALO, ny + 2 * HALO
    depth = ny // 8
    width = dirs + 256
    step = pl.program_id(0)
    sub = lax.broadcasted_iota(jnp.int32, (8, 128), 0)

    def at_cell(slot, t, v):
        return spread[slot, t, pl.ds(v, 8, depth + 1), :] if v < depth else spread[slot, t, ny + 8:ext_y + 8, :]

    def lay(slot, t, value):
        for y in range(0, ext_y, 8):
            at = y + y // depth if y < ny else y + 8
            spread[slot, t, at:at + 8, :] = value[y:y + 8]

    def widen(i, slot):
        rows = pl.ds(pl.multiple_of(i * PART, 2 * PART), 2 * PART)
        lhs = jnp.concatenate([stack[0, rows, :], stack[1, rows, :][:, :ext_y - 128]], axis=1).astype(BF16)
        wide = lax.dot_general(lhs, expand[...], TN, preferred_element_type=F32)
        for t in range(2 * width // 128):
            lay(slot, t, wide[:, 128 * t:128 * t + 128])

    @pl.when(step == 0)
    def _():
        total[...] = jnp.zeros_like(total)
        row = lax.broadcasted_iota(jnp.int32, (2 * PART, 2 * width), 0)
        col = lax.broadcasted_iota(jnp.int32, (2 * PART, 2 * width), 1)
        same = row // PART == col // width
        row, col = row % PART, col % width
        pick = (row < 24) & (row % 8 == col // PROBES) & (col < dirs)
        pick |= (row >= 24) & (row < 27) & (col >= dirs) & (col < dirs + 128)
        pick |= (row >= 27) & (row < 30) & (col >= dirs + 128)
        expand[...] = jnp.where(pick & same, 1.0, 0.0).astype(BF16)
        s = stiff_ref[...]
        stack[...] = jnp.zeros_like(stack)

        def put(value, at):
            where = pl.ds(at, ext_x, PART)
            stack[0, where, :] = value[:, :128]
            stack[1, where, :] = jnp.concatenate([value[:, 128:], jnp.zeros((ext_x, 256 - ext_y), F32)], axis=1)

        for g in range(shots):
            for part, value in enumerate(split3(field_ref[g, :ext_x, :] * s)):
                put(value, 8 * part + g)
        square = s * s
        for part, value in enumerate(split3(tau_step * square)):
            put(value, 24 + part)
        for part, value in enumerate(split3(1.0 / jnp.where(s > 0.0, square, 1.0))):
            put(value, 27 + part)
        words = jnp.concatenate(
            [field_ref[g, ext_x:ext_x + 8, :] for g in range(shots)], axis=0
        ).astype(BF16)
        row = lax.broadcasted_iota(jnp.int32, (8 * shots, dirs), 0)
        col = lax.broadcasted_iota(jnp.int32, (8 * shots, dirs), 1)

        def bits(offset, shift):
            probe = (col + shift) % PROBES
            hit = (row // 8 == col // PROBES) & (row % 8 - offset == probe // 8)
            value = lax.dot_general(words, jnp.where(hit, 1.0, 0.0).astype(BF16), TN, preferred_element_type=F32)
            lane = (lax.broadcasted_iota(jnp.int32, value.shape, 1) + shift) % 8
            bit = jnp.right_shift(value.astype(jnp.int32), lane) & 1
            return (2 * bit - 1).astype(F32)

        first[...] = bits(0, 0)[:ext_x]
        first_next[...] = 0.5 * bits(0, 1)[:ext_x]
        for ref, shift in ((second, 0), (second_next, 1)):
            value = bits(4, shift)
            for h in range(halves):
                lay(0, h, value[:, 128 * h:128 * h + 128])
                for v in range(depth + 1):
                    ref[h, v] = at_cell(0, h, v)
        widen(0, 0)

    pairs = ROWS // 2
    count = width // 128

    def place(row):
        return (row >> 1) & (pairs - 1), (row & 1) * count

    def stencil(src, at, emit):
        centre, upper, lower, edge = {}, {}, {}, {}
        for h in range(halves):
            for k in range(2):
                ref = src.at[(at + k) & 3, h]
                head, tail, halo = ref[0], ref[depth - 1], ref[depth]
                head_up, halo_up = pltpu.roll(head, 7, 0), pltpu.roll(halo, 7, 0)
                tail_down, halo_down = pltpu.roll(tail, 1, 0), pltpu.roll(halo, 1, 0)
                edge[h, k] = jnp.where(sub == 7, halo_up, head_up)
                after_halo = jnp.where(sub == 7, head_up, halo_up)
                before_head = jnp.where(sub == 0, halo_down, tail_down)
                before_halo = jnp.where(sub == 0, tail_down, halo_down)
                lower[h, k], centre[h, k] = before_head, head
                upper[h, k] = after_halo + before_halo
        for v in range(depth + 1):
            c = [at_cell(*[place(at + k)[0], place(at + k)[1] + halves], v) for k in range(2)]
            for h in range(halves):
                above = src[(at - 1) & 3, h, v]
                below = src[(at + 2) & 3, h, v]
                if v == depth:
                    for k in range(2):
                        centre[h, k] = src[(at + k) & 3, h, v]
                mid = [centre[h, k] for k in range(2)]
                for k in range(2):
                    if v < depth:
                        after = src[(at + k) & 3, h, v + 1] if v < depth - 1 else edge[h, k]
                        side = after + lower[h, k]
                        lower[h, k], centre[h, k] = mid[k], after
                    else:
                        side = upper[h, k]
                    beside = (above + mid[1]) if k == 0 else (mid[0] + below)
                    emit(k, h, v, mid[k] + c[k] * ((beside + side) - 4.0 * mid[k]))

    def level(src, at, dst):
        def emit(k, h, v, value):
            dst[(at + k) & 3, h, v] = value
        stencil(src, at, emit)

    for p in range(pairs):
        i = 2 * p
        first_row = [first[pl.ds(step * ROWS + i + k, 1), :] for k in range(2)]
        next_row = [first_next[pl.ds(step * ROWS + i + k, 1), :] for k in range(2)]
        for v in range(depth + 1):
            for h in range(halves):
                lanes = slice(128 * h, 128 * h + 128)
                one, two = second[h, v], second_next[h, v]
                for k in range(2):
                    probe = first_row[k][:, lanes] * one + next_row[k][:, lanes] * two
                    slot, tile = place(i + k)
                    w0[(i + k) & 3, h, v] = at_cell(slot, tile + h, v) * probe
        widen(jnp.minimum(step * ROWS + i + 2, ext_x - 2), (p + 1) % pairs)
        level(w0, i - 1, w1)
        level(w1, i - 2, w2)
        level(w2, i - 3, w3)

        def emit(k, h, v, value):
            if v < depth:
                slot, tile = place(i - 4 + k)
                scale = at_cell(slot, tile + h, v) * at_cell(slot, tile + halves + 1, v)
                fold[2 * h + k, 9 * v:9 * v + 8, :] = scale * value

        stencil(w3, i - 4, emit)
        for h in range(halves):
            for k in range(2):
                for q in range(0, depth, 2):
                    value = jnp.concatenate(
                        [fold[2 * h + k, pl.ds(9 * (r % depth) + r // depth, 8, 9), :] for r in (8 * q, 8 * q + 8)], axis=0
                    )
                    for part, piece in enumerate(split2(value)):
                        at_lane = part * dirs + 128 * h
                        parts_ref[i + k, 8 * q:8 * q + 16, at_lane:at_lane + 128] = piece

    @pl.when(step > 0)
    def _():
        parts = parts_ref[...].reshape(ROWS * ny, 2 * dirs)
        total[...] += lax.dot_general(parts[:, :dirs], parts, TN, preferred_element_type=F32)

    @pl.when(step == pl.num_programs(0) - 1)
    def _():
        cross = total[:, dirs:]
        total[:, :dirs] = total[:, :dirs] + cross + cross.T
        index = index_ref[0]
        strip = lambda at: total[pl.ds(pl.multiple_of(at * PROBES, PROBES), PROBES), :dirs]
        own_ref[...] = strip(index)
        other_ref[...] = strip(index ^ 1)


def responses(index, fields, stiffness, nx, ny):
    shots = fields.shape[0]
    dirs = shots * PROBES
    halves = dirs // 128
    ext_x, ext_y = nx + 2 * HALO, ny + 2 * HALO
    blocks = ext_y // 8
    width = dirs + 256
    whole = lambda shape: pl.BlockSpec(shape, lambda s: (0,) * len(shape))
    block = pl.BlockSpec((ROWS, ny, 2 * dirs), lambda s: (jnp.maximum(s - 1, 0), 0, 0))
    return pl.pallas_call(
        functools.partial(response_kernel, shots, nx, ny),
        grid=(ext_x // ROWS,),
        in_specs=[SMEM, whole(fields.shape), whole(stiffness.shape)],
        out_specs=[whole((PROBES, dirs)), whole((PROBES, dirs)), block],
        out_shape=[
            jax.ShapeDtypeStruct((PROBES, dirs), F32),
            jax.ShapeDtypeStruct((PROBES, dirs), F32),
            jax.ShapeDtypeStruct((nx, ny, 2 * dirs), BF16),
        ],
        scratch_shapes=[
            pltpu.VMEM((2 * PART, 2 * width), BF16),
            pltpu.VMEM((2, ext_x * PART, 128), F32),
            pltpu.VMEM((ROWS // 2, 2 * width // 128, ext_y + 8, 128), F32),
            pltpu.VMEM((ext_x, dirs), F32),
            pltpu.VMEM((ext_x, dirs), F32),
            pltpu.VMEM((halves, blocks, 8, 128), F32),
            pltpu.VMEM((halves, blocks, 8, 128), F32),
            *[pltpu.VMEM((4, halves, blocks, 8, 128), F32) for _ in range(4)],
            pltpu.VMEM((2 * halves, ny + 2 * 8, 128), F32),
            pltpu.VMEM((dirs, 2 * dirs), F32),
        ],
        compiler_params=pltpu.CompilerParams(
            dimension_semantics=("arbitrary",), vmem_limit_bytes=61 * 2**20
        ),
        name="responses",
    )(index, fields, stiffness)


PANEL = 64
PIVOT = 8


def cholesky(n, gram_ref, table):
    tiles = n // 128
    eye_row = lax.broadcasted_iota(jnp.int32, (8, 128), 0)
    eye_col = lax.broadcasted_iota(jnp.int32, (8, 128), 1)
    table[:, :n] = gram_ref[...]
    full = lambda x: jnp.broadcast_to(x, (8, 128))
    for panel in range(n // PANEL):
        start = panel * PANEL
        tile = start // 128
        live = [*range(tile, tiles), *range(tiles, tiles + tile + 1)]
        rows = {}
        for g in range(PANEL // 8):
            for t in live:
                at = start + 8 * g
                value = None
                if t < tiles or panel > 0:
                    value = table[at:at + 8, 128 * t:128 * t + 128] if (t < tiles or (t - tiles) * 128 < start) else None
                if t >= tiles:
                    unit = (eye_row + at == eye_col + 128 * (t - tiles)).astype(F32)
                    value = unit if value is None else value + unit
                rows[g, t] = value
        for micro in range(PANEL // PIVOT):
            k = micro * PIVOT
            gp, r = k // 8, k % 8
            lane = (start + k) % 128
            pivot_rows = [{t: full(rows[gp, t][r + j:r + j + 1, :]) for t in live} for j in range(PIVOT)]
            a = {
                (i, j): full(pivot_rows[i][tile][:, lane + j:lane + j + 1])
                for i in range(PIVOT) for j in range(i + 1)
            }
            low, inv = {}, []
            for j in range(PIVOT):
                d = a[j, j]
                for m in range(j):
                    d = d - low[j, m] * low[j, m]
                inv.append(lax.rsqrt(d))
                for i in range(j + 1, PIVOT):
                    v = a[i, j]
                    for m in range(j):
                        v = v - low[i, m] * low[j, m]
                    low[i, j] = v * inv[j]
            ready = []
            for j in range(PIVOT):
                out = {}
                for t in live:
                    v = pivot_rows[j][t]
                    for m in range(j):
                        v = v - low[j, m] * ready[m][t]
                    out[t] = v * inv[j]
                ready.append(out)
            for g in range(gp, PANEL // 8):
                if g == gp and r + PIVOT == 8:
                    pass
                else:
                    cols = []
                    for j in range(PIVOT):
                        v = full(rows[g, tile][:, lane + j:lane + j + 1])
                        for m in range(j):
                            v = v - cols[m] * low[j, m]
                        cols.append(v * inv[j])
                    if g == gp:
                        cols = [jnp.where(eye_row >= r + PIVOT, v, 0.0) for v in cols]
                    for t in live:
                        v = rows[g, t]
                        for j in range(PIVOT):
                            v = v - cols[j] * ready[j][t]
                        rows[g, t] = v
                if g == gp:
                    for t in live:
                        v = rows[g, t]
                        for j in range(PIVOT):
                            v = jnp.where(eye_row == r + j, ready[j][t], v)
                        rows[g, t] = v
        for g in range(PANEL // 8):
            for t in live:
                at = start + 8 * g
                value = rows[g, t]
                if t == tile:
                    value = jnp.where(eye_row + at <= eye_col + 128 * t, value, 0.0)
                table[at:at + 8, 128 * t:128 * t + 128] = value
            for t in range(tile):
                table[start + 8 * g:start + 8 * g + 8, 128 * t:128 * t + 128] = jnp.zeros((8, 128), F32)
            for t in range(tiles + tile + 1, 2 * tiles):
                table[start + 8 * g:start + 8 * g + 8, 128 * t:128 * t + 128] = jnp.zeros((8, 128), F32)
        below = start + PANEL
        if below < n:
            keep = below // 128
            for t in range(keep, tiles + tile + 1):
                if t == keep:
                    lo = 128 * keep
                    left = table[start:below, lo:n]
                    p3 = [v.astype(BF16) for v in split3(left)]
                    lhs = jnp.concatenate([p3[0], p3[0], p3[1], p3[0], p3[2], p3[1]], axis=0)
                lanes = slice(128 * t, 128 * t + 128)
                right = [v.astype(BF16) for v in split3(table[start:below, lanes])]
                rhs = jnp.concatenate([right[0], right[1], right[0], right[2], right[0], right[1]], axis=0)
                update = lax.dot_general(lhs, rhs, TN, preferred_element_type=F32)[below - lo:]
                if t < tiles or 128 * (t - tiles) < start:
                    table[below:, lanes] = table[below:, lanes] - update
                else:
                    table[below:, lanes] = -update

def finish_kernel(n, scale, index_ref, gram_ref, parts_any, upper_ref, own_ref, other_ref, table, parts_ref, sem):
    copy = pltpu.make_async_copy(parts_any, parts_ref, sem)
    copy.start()
    cholesky(n, gram_ref, table)
    index = index_ref[0]
    strip = lambda at: pl.ds(pl.multiple_of(at * PROBES, PROBES), PROBES)
    upper_ref[...] = table[strip(index), :n] * (1.0 / scale)
    rows = jnp.concatenate([table[strip(index), n:], table[strip(index ^ 1), n:]], axis=0) * scale
    high, low = split2(rows)
    both = jnp.concatenate([high, low], axis=0)
    copy.wait()
    count, ny = parts_ref.shape[:2]
    for i in range(0, count, 2):
        parts = parts_ref[i:i + 2].reshape(2 * ny, 2 * n)
        main = lax.dot_general(both, parts[:, :n], NT, preferred_element_type=F32)
        rest = lax.dot_general(high, parts[:, n:], NT, preferred_element_type=F32)
        value = main[:2 * PROBES] + (main[2 * PROBES:] + rest)
        for k in range(2):
            own_ref[:, i + k, :] = value[:PROBES, ny * k:ny * k + ny]
            other_ref[:, i + k, :] = value[PROBES:, ny * k:ny * k + ny]


def finish(index, gram, parts, scale):
    n = gram.shape[0]
    nx, ny = parts.shape[:2]
    return pl.pallas_call(
        functools.partial(finish_kernel, n, scale),
        in_specs=[SMEM, VMEM, pl.BlockSpec(memory_space=pl.ANY)],
        out_specs=[VMEM] * 3,
        out_shape=[
            jax.ShapeDtypeStruct((PROBES, n), F32),
            jax.ShapeDtypeStruct((PROBES, nx, ny), F32),
            jax.ShapeDtypeStruct((PROBES, nx, ny), F32),
        ],
        scratch_shapes=[
            pltpu.VMEM((n, 2 * n), F32),
            pltpu.VMEM(parts.shape, BF16),
            pltpu.SemaphoreType.DMA,
        ],
        compiler_params=pltpu.CompilerParams(vmem_limit_bytes=16 * 2**20),
        name="finish",
    )(index, gram, parts)


def shards(signs_x, signs_y, heights, velocity, background):
    shots = lax.axis_size("dir")
    nx, ny = background.shape[1:]
    ext_x, ext_y = nx + 2 * HALO, ny + 2 * HALO
    half = nx // 2
    index = lax.axis_index("dir")
    which = index.reshape(1)
    stiffness, first, last = small(
        pack_x_kernel, [(nx, ny), (16, ny), (16, ny)], [VMEM] * 4, "pack_x", 60
    )(signs_x, heights, velocity, background)
    above, below = exchange(first, last, "sx")
    field, stiffness, octets, first, last = small(
        pack_y_kernel, [(ext_x, ny), (ext_x, ny), (8, ny), (ext_x + 8, ny), (ext_x + 8, ny)], [VMEM] * 6, "pack_y"
    )(signs_y, background, stiffness, first, above, below)
    left, right = exchange(first, last, "sy")
    send, stiffness = small(
        pack_dir_kernel, [(shots, half + 2 * HALO + 8, ext_y), (half + 2 * HALO, ext_y)], [SMEM] + [VMEM] * 6, "pack_dir"
    )(which, field, stiffness, octets, first, left, right)
    fields = lax.all_to_all(send, "dir", 0, 0)
    own, other, parts = responses(which, fields, stiffness, half, ny)
    swap = [(i, i ^ 1) for i in range(shots)]
    dirs = shots * PROBES
    strip = own + lax.ppermute(other, "dir", swap)
    terms = lax.all_to_all(strip.reshape(PROBES, dirs // 128, 128), ("sx", "sy"), 0, 0)
    row = jnp.sum(terms, axis=0, keepdims=True)
    gram = lax.all_to_all(jnp.broadcast_to(row, (dirs, *row.shape[1:])), ("dir", "sx", "sy"), 0, 0)
    gram = gram.reshape(dirs, dirs)
    scale = math.sqrt(nx * ny * lax.axis_size("sx") * lax.axis_size("sy"))
    factor, own, other = finish(which, gram, parts, scale)
    other = lax.ppermute(other, "dir", swap)
    upper = index & 1 == 1
    basis = jnp.concatenate([jnp.where(upper, other, own), jnp.where(upper, own, other)], axis=1)
    return basis, factor


def solution(mesh):
    in_specs = (P("dir", "sx"), P("dir", "sy"), P("sx", "sy"), P("sx", "sy"), P("dir", "sx", "sy"))
    out_specs = (P("dir", "sx", "sy"), P("dir", None))
    return jax.shard_map(shards, mesh=mesh, in_specs=in_specs, out_specs=out_specs, check_vma=False)
```

```python
import functools
import math

import jax
import jax.numpy as jnp
from jax import lax
from jax.experimental import pallas as pl
from jax.experimental.pallas import tpu as pltpu
from jax.sharding import PartitionSpec as P

PROBES = 32
LEVELS = 64
HALO = 4
ROWS = 8
tau_step = 0.02

F32 = jnp.float32
BF16 = jnp.bfloat16
TN = (((0,), (0,)), ((), ()))
NT = (((1,), (1,)), ((), ()))
VMEM = pl.BlockSpec(memory_space=pltpu.VMEM)
SMEM = pl.BlockSpec(memory_space=pltpu.SMEM)


def split2(x):
    high = x.astype(BF16)
    return high, (x - high.astype(F32)).astype(BF16)


def split3(x):
    high = x.astype(BF16).astype(F32)
    rest = x - high
    mid = rest.astype(BF16).astype(F32)
    return high, mid, rest - mid


def sign_bytes(words):
    shape = (8, words.shape[1])
    shift = 8 * (lax.broadcasted_iota(jnp.int32, shape, 0) & 3)
    return (jnp.right_shift(jnp.broadcast_to(words, shape), shift) & 255).astype(F32)


def pack_x_kernel(signs_ref, other_signs_ref, heights_ref, velocity_ref, field_ref, body_ref, first_ref, last_ref):
    nx, ny = velocity_ref.shape
    stiff = velocity_ref[...] * jnp.sqrt(1.0 + heights_ref[...].astype(F32) / LEVELS)
    octets = sign_bytes(signs_ref[...])
    body_ref[0:nx, :] = field_ref[0]
    body_ref[nx:2 * nx, :] = stiff
    body_ref[2 * nx:2 * nx + 8, :] = jnp.zeros((8, ny), F32)
    body_ref[2 * nx:2 * nx + 8, :nx] = octets
    body_ref[2 * nx + 8:, :] = sign_bytes(other_signs_ref[...])
    for ref, start in ((first_ref, 0), (last_ref, nx - HALO)):
        ref[0:HALO, :] = field_ref[0, start:start + HALO, :]
        ref[HALO:2 * HALO, :] = stiff[start:start + HALO]
        ref[8:16, :] = jnp.zeros((8, ny), F32)
        ref[8:16, :nx] = octets


def pack_y_kernel(body_ref, above_ref, below_ref,
                  field_out, stiff_out, octets_out, first_ref, last_ref):
    nx, ny = (body_ref.shape[0] - 16) // 2, body_ref.shape[1]
    ext_x = nx + 2 * HALO
    field_out[0:HALO, :] = above_ref[0:HALO, :]
    field_out[HALO:HALO + nx, :] = body_ref[0:nx, :]
    field_out[HALO + nx:ext_x, :] = below_ref[0:HALO, :]
    stiff_out[0:HALO, :] = above_ref[HALO:2 * HALO, :]
    stiff_out[HALO:HALO + nx, :] = body_ref[nx:2 * nx, :]
    stiff_out[HALO + nx:ext_x, :] = below_ref[HALO:2 * HALO, :]
    lane = lax.broadcasted_iota(jnp.int32, (8, ny), 1)
    after = pltpu.roll(below_ref[8:16, :], nx + HALO, 1)
    before = pltpu.roll(above_ref[8:16, :], ny - nx + HALO, 1)
    own = pltpu.roll(body_ref[2 * nx:2 * nx + 8, :], HALO, 1)
    octets_out[...] = jnp.where(lane < HALO, before, jnp.where(lane < HALO + nx, own, after))
    octets = body_ref[2 * nx + 8:, :]
    field, stiff = field_out[...], stiff_out[...]
    lane = lax.broadcasted_iota(jnp.int32, field.shape, 1)
    first_ref[0:ext_x, :] = jnp.where(lane < HALO, field, pltpu.roll(stiff, HALO, 1))
    first_ref[ext_x:, :] = octets
    last_ref[0:ext_x, :] = jnp.where(lane < 2 * HALO, pltpu.roll(field, 2 * HALO, 1), pltpu.roll(stiff, 3 * HALO, 1))
    last_ref[ext_x:, :] = octets


def pack_dir_kernel(index_ref, field_ref, stiff_ref, octets_ref, own_ref, left_ref, right_ref, send_ref, stiff_out):
    ext_x, ny = field_ref.shape
    half = (ext_x - 2 * HALO) // 2
    take = half + 2 * HALO
    left, right = left_ref[0:ext_x, :], right_ref[0:ext_x, :]
    lane = lax.broadcasted_iota(jnp.int32, left.shape, 1)
    field_side = jnp.where(lane < HALO, right, left)
    shift = lambda v: pltpu.roll(v, ny - HALO, 1)
    stiff_side = jnp.where(lane < HALO, shift(right), shift(left))
    lane = lax.broadcasted_iota(jnp.int32, (8, ny), 1)
    octet_side = jnp.where(lane < HALO, right_ref[ext_x:, :], pltpu.roll(left_ref[ext_x:, :], 2 * HALO, 1))
    own_octets = own_ref[ext_x:, :]
    for dest in range(send_ref.shape[0]):
        part = dest & 1
        rows = slice(part * half, part * half + take)
        send_ref[dest, 0:take, 0:ny] = field_ref[rows, :]
        send_ref[dest, 0:take, ny:] = field_side[rows, :2 * HALO]
        x_octets = octets_ref[...] if part == 0 else pltpu.roll(octets_ref[...], ny - half, 1)
        send_ref[dest, take:take + 4, 0:ny] = x_octets[0:4]
        send_ref[dest, take:take + 4, ny:] = jnp.zeros((4, 2 * HALO), F32)
        send_ref[dest, take + 4:take + 8, 0:ny] = own_octets[0:4]
        send_ref[dest, take + 4:take + 8, ny:] = octet_side[0:4, :2 * HALO]
    row = pl.multiple_of((index_ref[0] & 1) * half, half)
    stiff_out[:, 0:ny] = stiff_ref[pl.ds(row, take), :]
    spare = jnp.where(index_ref[0] & 1 == 1, stiff_side[half:half + take], stiff_side[0:take])
    stiff_out[:, ny:] = spare[:, :2 * HALO]


def small(kernel, shapes, specs, name, limit=4):
    return pl.pallas_call(
        kernel,
        in_specs=specs,
        out_specs=[VMEM] * len(shapes),
        out_shape=[jax.ShapeDtypeStruct(shape, F32) for shape in shapes],
        compiler_params=pltpu.CompilerParams(vmem_limit_bytes=limit * 2**20),
        name=name,
    )


def exchange(first, last, axis):
    count = lax.axis_size(axis)
    before = lax.ppermute(last, axis, [(i, i + 1) for i in range(count - 1)])
    after = lax.ppermute(first, axis, [(i + 1, i) for i in range(count - 1)])
    return before, after


PART = 32


def response_kernel(shots, nx, ny, index_ref, field_ref, stiff_ref, own_ref, other_ref, parts_ref,
                    expand, stack, spread, first, first_next, second, second_next,
                    w0, w1, w2, w3, fold, total):
    dirs = shots * PROBES
    halves = dirs // 128
    ext_x, ext_y = nx + 2 * HALO, ny + 2 * HALO
    depth = ny // 8
    width = dirs + 256
    step = pl.program_id(0)
    sub = lax.broadcasted_iota(jnp.int32, (8, 128), 0)

    def at_cell(slot, t, v):
        return spread[slot, t, pl.ds(v, 8, depth + 1), :] if v < depth else spread[slot, t, ny + 8:ext_y + 8, :]

    def lay(slot, t, value):
        for y in range(0, ext_y, 8):
            at = y + y // depth if y < ny else y + 8
            spread[slot, t, at:at + 8, :] = value[y:y + 8]

    def widen(i, slot):
        rows = pl.ds(pl.multiple_of(i * PART, 2 * PART), 2 * PART)
        lhs = jnp.concatenate([stack[0, rows, :], stack[1, rows, :][:, :ext_y - 128]], axis=1).astype(BF16)
        wide = lax.dot_general(lhs, expand[...], TN, preferred_element_type=F32)
        for t in range(2 * width // 128):
            lay(slot, t, wide[:, 128 * t:128 * t + 128])

    @pl.when(step == 0)
    def _():
        total[...] = jnp.zeros_like(total)
        row = lax.broadcasted_iota(jnp.int32, (2 * PART, 2 * width), 0)
        col = lax.broadcasted_iota(jnp.int32, (2 * PART, 2 * width), 1)
        same = row // PART == col // width
        row, col = row % PART, col % width
        pick = (row < 24) & (row % 8 == col // PROBES) & (col < dirs)
        pick |= (row >= 24) & (row < 27) & (col >= dirs) & (col < dirs + 128)
        pick |= (row >= 27) & (row < 30) & (col >= dirs + 128)
        expand[...] = jnp.where(pick & same, 1.0, 0.0).astype(BF16)
        s = stiff_ref[...]
        stack[...] = jnp.zeros_like(stack)

        def put(value, at):
            where = pl.ds(at, ext_x, PART)
            stack[0, where, :] = value[:, :128]
            stack[1, where, :] = jnp.concatenate([value[:, 128:], jnp.zeros((ext_x, 256 - ext_y), F32)], axis=1)

        for g in range(shots):
            for part, value in enumerate(split3(field_ref[g, :ext_x, :] * s)):
                put(value, 8 * part + g)
        square = s * s
        for part, value in enumerate(split3(tau_step * square)):
            put(value, 24 + part)
        for part, value in enumerate(split3(1.0 / jnp.where(s > 0.0, square, 1.0))):
            put(value, 27 + part)
        words = jnp.concatenate(
            [field_ref[g, ext_x:ext_x + 8, :] for g in range(shots)], axis=0
        ).astype(BF16)
        row = lax.broadcasted_iota(jnp.int32, (8 * shots, dirs), 0)
        col = lax.broadcasted_iota(jnp.int32, (8 * shots, dirs), 1)

        def bits(offset, shift):
            probe = (col + shift) % PROBES
            hit = (row // 8 == col // PROBES) & (row % 8 - offset == probe // 8)
            value = lax.dot_general(words, jnp.where(hit, 1.0, 0.0).astype(BF16), TN, preferred_element_type=F32)
            lane = (lax.broadcasted_iota(jnp.int32, value.shape, 1) + shift) % 8
            bit = jnp.right_shift(value.astype(jnp.int32), lane) & 1
            return (2 * bit - 1).astype(F32)

        first[...] = bits(0, 0)[:ext_x]
        first_next[...] = 0.5 * bits(0, 1)[:ext_x]
        for ref, shift in ((second, 0), (second_next, 1)):
            value = bits(4, shift)
            for h in range(halves):
                lay(0, h, value[:, 128 * h:128 * h + 128])
                for v in range(depth + 1):
                    ref[h, v] = at_cell(0, h, v)
        widen(0, 0)

    pairs = ROWS // 2
    count = width // 128

    def place(row):
        return (row >> 1) & (pairs - 1), (row & 1) * count

    def stencil(src, at, emit):
        centre, upper, lower, edge = {}, {}, {}, {}
        for h in range(halves):
            for k in range(2):
                ref = src.at[(at + k) & 3, h]
                head, tail, halo = ref[0], ref[depth - 1], ref[depth]
                head_up, halo_up = pltpu.roll(head, 7, 0), pltpu.roll(halo, 7, 0)
                tail_down, halo_down = pltpu.roll(tail, 1, 0), pltpu.roll(halo, 1, 0)
                edge[h, k] = jnp.where(sub == 7, halo_up, head_up)
                after_halo = jnp.where(sub == 7, head_up, halo_up)
                before_head = jnp.where(sub == 0, halo_down, tail_down)
                before_halo = jnp.where(sub == 0, tail_down, halo_down)
                lower[h, k], centre[h, k] = before_head, head
                upper[h, k] = after_halo + before_halo
        for v in range(depth + 1):
            c = [at_cell(*[place(at + k)[0], place(at + k)[1] + halves], v) for k in range(2)]
            for h in range(halves):
                above = src[(at - 1) & 3, h, v]
                below = src[(at + 2) & 3, h, v]
                if v == depth:
                    for k in range(2):
                        centre[h, k] = src[(at + k) & 3, h, v]
                mid = [centre[h, k] for k in range(2)]
                for k in range(2):
                    if v < depth:
                        after = src[(at + k) & 3, h, v + 1] if v < depth - 1 else edge[h, k]
                        side = after + lower[h, k]
                        lower[h, k], centre[h, k] = mid[k], after
                    else:
                        side = upper[h, k]
                    beside = (above + mid[1]) if k == 0 else (mid[0] + below)
                    emit(k, h, v, mid[k] + c[k] * ((beside + side) - 4.0 * mid[k]))

    def level(src, at, dst):
        def emit(k, h, v, value):
            dst[(at + k) & 3, h, v] = value
        stencil(src, at, emit)

    for p in range(pairs):
        i = 2 * p
        first_row = [first[pl.ds(step * ROWS + i + k, 1), :] for k in range(2)]
        next_row = [first_next[pl.ds(step * ROWS + i + k, 1), :] for k in range(2)]
        for v in range(depth + 1):
            for h in range(halves):
                lanes = slice(128 * h, 128 * h + 128)
                one, two = second[h, v], second_next[h, v]
                for k in range(2):
                    probe = first_row[k][:, lanes] * one + next_row[k][:, lanes] * two
                    slot, tile = place(i + k)
                    w0[(i + k) & 3, h, v] = at_cell(slot, tile + h, v) * probe
        widen(jnp.minimum(step * ROWS + i + 2, ext_x - 2), (p + 1) % pairs)
        level(w0, i - 1, w1)
        level(w1, i - 2, w2)
        level(w2, i - 3, w3)

        def emit(k, h, v, value):
            if v < depth:
                slot, tile = place(i - 4 + k)
                scale = at_cell(slot, tile + h, v) * at_cell(slot, tile + halves + 1, v)
                fold[2 * h + k, 9 * v:9 * v + 8, :] = scale * value

        stencil(w3, i - 4, emit)
        for h in range(halves):
            for k in range(2):
                for q in range(0, depth, 2):
                    value = jnp.concatenate(
                        [fold[2 * h + k, pl.ds(9 * (r % depth) + r // depth, 8, 9), :] for r in (8 * q, 8 * q + 8)], axis=0
                    )
                    for part, piece in enumerate(split2(value)):
                        at_lane = part * dirs + 128 * h
                        parts_ref[i + k, 8 * q:8 * q + 16, at_lane:at_lane + 128] = piece

    @pl.when(step > 0)
    def _():
        parts = parts_ref[...].reshape(ROWS * ny, 2 * dirs)
        total[...] += lax.dot_general(parts[:, :dirs], parts, TN, preferred_element_type=F32)

    @pl.when(step == pl.num_programs(0) - 1)
    def _():
        cross = total[:, dirs:]
        total[:, :dirs] = total[:, :dirs] + cross + cross.T
        index = index_ref[0]
        strip = lambda at: total[pl.ds(pl.multiple_of(at * PROBES, PROBES), PROBES), :dirs]
        own_ref[...] = strip(index)
        other_ref[...] = strip(index ^ 1)


def responses(index, fields, stiffness, nx, ny):
    shots = fields.shape[0]
    dirs = shots * PROBES
    halves = dirs // 128
    ext_x, ext_y = nx + 2 * HALO, ny + 2 * HALO
    blocks = ext_y // 8
    width = dirs + 256
    whole = lambda shape: pl.BlockSpec(shape, lambda s: (0,) * len(shape))
    block = pl.BlockSpec((ROWS, ny, 2 * dirs), lambda s: (jnp.maximum(s - 1, 0), 0, 0))
    return pl.pallas_call(
        functools.partial(response_kernel, shots, nx, ny),
        grid=(ext_x // ROWS,),
        in_specs=[SMEM, whole(fields.shape), whole(stiffness.shape)],
        out_specs=[whole((PROBES, dirs)), whole((PROBES, dirs)), block],
        out_shape=[
            jax.ShapeDtypeStruct((PROBES, dirs), F32),
            jax.ShapeDtypeStruct((PROBES, dirs), F32),
            jax.ShapeDtypeStruct((nx, ny, 2 * dirs), BF16),
        ],
        scratch_shapes=[
            pltpu.VMEM((2 * PART, 2 * width), BF16),
            pltpu.VMEM((2, ext_x * PART, 128), F32),
            pltpu.VMEM((ROWS // 2, 2 * width // 128, ext_y + 8, 128), F32),
            pltpu.VMEM((ext_x, dirs), F32),
            pltpu.VMEM((ext_x, dirs), F32),
            pltpu.VMEM((halves, blocks, 8, 128), F32),
            pltpu.VMEM((halves, blocks, 8, 128), F32),
            *[pltpu.VMEM((4, halves, blocks, 8, 128), F32) for _ in range(4)],
            pltpu.VMEM((2 * halves, ny + 2 * 8, 128), F32),
            pltpu.VMEM((dirs, 2 * dirs), F32),
        ],
        compiler_params=pltpu.CompilerParams(
            dimension_semantics=("arbitrary",), vmem_limit_bytes=52 * 2**20
        ),
        name="responses",
    )(index, fields, stiffness)


PANEL = 64
PIVOT = 8


def cholesky(n, gram_ref, table):
    tiles = n // 128
    eye_row = lax.broadcasted_iota(jnp.int32, (8, 128), 0)
    eye_col = lax.broadcasted_iota(jnp.int32, (8, 128), 1)
    table[:, :n] = gram_ref[...]
    full = lambda x: jnp.broadcast_to(x, (8, 128))
    for panel in range(n // PANEL):
        start = panel * PANEL
        tile = start // 128
        live = [*range(tile, tiles), *range(tiles, tiles + tile + 1)]
        rows = {}
        for g in range(PANEL // 8):
            for t in live:
                at = start + 8 * g
                value = None
                if t < tiles or panel > 0:
                    value = table[at:at + 8, 128 * t:128 * t + 128] if (t < tiles or (t - tiles) * 128 < start) else None
                if t >= tiles:
                    unit = (eye_row + at == eye_col + 128 * (t - tiles)).astype(F32)
                    value = unit if value is None else value + unit
                rows[g, t] = value
        for micro in range(PANEL // PIVOT):
            k = micro * PIVOT
            gp, r = k // 8, k % 8
            lane = (start + k) % 128
            pivot_rows = [{t: full(rows[gp, t][r + j:r + j + 1, :]) for t in live} for j in range(PIVOT)]
            a = {
                (i, j): full(pivot_rows[i][tile][:, lane + j:lane + j + 1])
                for i in range(PIVOT) for j in range(i + 1)
            }
            low, inv = {}, []
            for j in range(PIVOT):
                d = a[j, j]
                for m in range(j):
                    d = d - low[j, m] * low[j, m]
                inv.append(lax.rsqrt(d))
                for i in range(j + 1, PIVOT):
                    v = a[i, j]
                    for m in range(j):
                        v = v - low[i, m] * low[j, m]
                    low[i, j] = v * inv[j]
            ready = []
            for j in range(PIVOT):
                out = {}
                for t in live:
                    v = pivot_rows[j][t]
                    for m in range(j):
                        v = v - low[j, m] * ready[m][t]
                    out[t] = v * inv[j]
                ready.append(out)
            for g in range(gp, PANEL // 8):
                if g == gp and r + PIVOT == 8:
                    pass
                else:
                    cols = []
                    for j in range(PIVOT):
                        v = full(rows[g, tile][:, lane + j:lane + j + 1])
                        for m in range(j):
                            v = v - cols[m] * low[j, m]
                        cols.append(v * inv[j])
                    if g == gp:
                        cols = [jnp.where(eye_row >= r + PIVOT, v, 0.0) for v in cols]
                    for t in live:
                        v = rows[g, t]
                        for j in range(PIVOT):
                            v = v - cols[j] * ready[j][t]
                        rows[g, t] = v
                if g == gp:
                    for t in live:
                        v = rows[g, t]
                        for j in range(PIVOT):
                            v = jnp.where(eye_row == r + j, ready[j][t], v)
                        rows[g, t] = v
        for g in range(PANEL // 8):
            for t in live:
                at = start + 8 * g
                value = rows[g, t]
                if t == tile:
                    value = jnp.where(eye_row + at <= eye_col + 128 * t, value, 0.0)
                table[at:at + 8, 128 * t:128 * t + 128] = value
            for t in range(tile):
                table[start + 8 * g:start + 8 * g + 8, 128 * t:128 * t + 128] = jnp.zeros((8, 128), F32)
            for t in range(tiles + tile + 1, 2 * tiles):
                table[start + 8 * g:start + 8 * g + 8, 128 * t:128 * t + 128] = jnp.zeros((8, 128), F32)
        below = start + PANEL
        if below < n:
            keep = below // 128
            for t in range(keep, tiles + tile + 1):
                if t == keep:
                    lo = 128 * keep
                    left = table[start:below, lo:n]
                    p3 = [v.astype(BF16) for v in split3(left)]
                    lhs = jnp.concatenate([p3[0], p3[0], p3[1], p3[0], p3[2], p3[1]], axis=0)
                lanes = slice(128 * t, 128 * t + 128)
                right = [v.astype(BF16) for v in split3(table[start:below, lanes])]
                rhs = jnp.concatenate([right[0], right[1], right[0], right[2], right[0], right[1]], axis=0)
                update = lax.dot_general(lhs, rhs, TN, preferred_element_type=F32)[below - lo:]
                if t < tiles or 128 * (t - tiles) < start:
                    table[below:, lanes] = table[below:, lanes] - update
                else:
                    table[below:, lanes] = -update

def finish_kernel(n, scale, index_ref, gram_ref, parts_any, upper_ref, own_ref, other_ref, table, parts_ref, sem):
    copy = pltpu.make_async_copy(parts_any, parts_ref, sem)
    copy.start()
    cholesky(n, gram_ref, table)
    index = index_ref[0]
    strip = lambda at: pl.ds(pl.multiple_of(at * PROBES, PROBES), PROBES)
    upper_ref[...] = table[strip(index), :n] * (1.0 / scale)
    rows = jnp.concatenate([table[strip(index), n:], table[strip(index ^ 1), n:]], axis=0) * scale
    high, low = split2(rows)
    both = jnp.concatenate([high, low], axis=0)
    copy.wait()
    count, ny = parts_ref.shape[:2]
    for i in range(0, count, 2):
        parts = parts_ref[i:i + 2].reshape(2 * ny, 2 * n)
        main = lax.dot_general(both, parts[:, :n], NT, preferred_element_type=F32)
        rest = lax.dot_general(high, parts[:, n:], NT, preferred_element_type=F32)
        value = main[:2 * PROBES] + (main[2 * PROBES:] + rest)
        for k in range(2):
            own_ref[:, i + k, :] = value[:PROBES, ny * k:ny * k + ny]
            other_ref[:, i + k, :] = value[PROBES:, ny * k:ny * k + ny]


def finish(index, gram, parts, scale):
    n = gram.shape[0]
    nx, ny = parts.shape[:2]
    return pl.pallas_call(
        functools.partial(finish_kernel, n, scale),
        in_specs=[SMEM, VMEM, pl.BlockSpec(memory_space=pl.ANY)],
        out_specs=[VMEM] * 3,
        out_shape=[
            jax.ShapeDtypeStruct((PROBES, n), F32),
            jax.ShapeDtypeStruct((PROBES, nx, ny), F32),
            jax.ShapeDtypeStruct((PROBES, nx, ny), F32),
        ],
        scratch_shapes=[
            pltpu.VMEM((n, 2 * n), F32),
            pltpu.VMEM(parts.shape, BF16),
            pltpu.SemaphoreType.DMA,
        ],
        compiler_params=pltpu.CompilerParams(vmem_limit_bytes=52 * 2**20),
        name="finish",
    )(index, gram, parts)


def shards(signs_x, signs_y, heights, velocity, background):
    shots = lax.axis_size("dir")
    nx, ny = background.shape[1:]
    ext_x, ext_y = nx + 2 * HALO, ny + 2 * HALO
    half = nx // 2
    index = lax.axis_index("dir")
    which = index.reshape(1)
    body, first, last = small(
        pack_x_kernel, [(2 * nx + 16, ny), (16, ny), (16, ny)], [VMEM] * 5, "pack_x", 60
    )(signs_x, signs_y, heights, velocity, background)
    above, below = exchange(first, last, "sx")
    field, stiffness, octets, first, last = small(
        pack_y_kernel, [(ext_x, ny), (ext_x, ny), (8, ny), (ext_x + 8, ny), (ext_x + 8, ny)], [VMEM] * 3, "pack_y"
    )(body, above, below)
    left, right = exchange(first, last, "sy")
    send, stiffness = small(
        pack_dir_kernel, [(shots, half + 2 * HALO + 8, ext_y), (half + 2 * HALO, ext_y)], [SMEM] + [VMEM] * 6, "pack_dir"
    )(which, field, stiffness, octets, first, left, right)
    fields = lax.all_to_all(send, "dir", 0, 0)
    own, other, parts = responses(which, fields, stiffness, half, ny)
    swap = [(i, i ^ 1) for i in range(shots)]
    dirs = shots * PROBES
    strip = own + lax.ppermute(other, "dir", swap)
    terms = lax.all_to_all(strip.reshape(PROBES, dirs // 128, 128), ("sx", "sy"), 0, 0)
    row = jnp.sum(terms, axis=0, keepdims=True)
    gram = lax.all_to_all(jnp.broadcast_to(row, (dirs, *row.shape[1:])), ("dir", "sx", "sy"), 0, 0)
    gram = gram.reshape(dirs, dirs)
    scale = math.sqrt(nx * ny * lax.axis_size("sx") * lax.axis_size("sy"))
    factor, own, other = finish(which, gram, parts, scale)
    other = lax.ppermute(other, "dir", swap)
    upper = index & 1 == 1
    basis = jnp.concatenate([jnp.where(upper, other, own), jnp.where(upper, own, other)], axis=1)
    return basis, factor


def solution(mesh):
    in_specs = (P("dir", "sx"), P("dir", "sy"), P("sx", "sy"), P("sx", "sy"), P("dir", "sx", "sy"))
    out_specs = (P("dir", "sx", "sy"), P("dir", None))
    return jax.shard_map(shards, mesh=mesh, in_specs=in_specs, out_specs=out_specs, check_vma=False)
```
